256 devices in a mesh: pipe: 8 (over x, core), expert: 32 (over y, z).
Axes of the slice: x: 4, y: 4, z: 8, core: 2. Of those that a mesh axis runs over, the one named last changes fastest.
Arguments:
- stream_fwd: bfloat16 [8, 4096, 3584], P('pipe', 'expert'), may hold values from -6 to 6
- stream_rev: bfloat16 [8, 4096, 3584], P('pipe', 'expert'), may hold values from -6 to 6
- norm_gain: bfloat16 [8, 3584], P('pipe'), may hold values from 0.099609375 to 1.8984375
- w_up: bfloat16 [8, 32, 3584, 512], P('pipe', 'expert'), may hold values from -0.09375 to 0.09375
- w_down: bfloat16 [8, 32, 512, 3584], P('pipe', 'expert'), may hold values from -0.1875 to 0.1875
- routes: int32 [8, 2, 4096, 2], P('pipe', None, 'expert'), may hold values from 0 to 15, all different within a row; in each aligned block of 128 rows (0 to 127, 128 to 255, ..., all dimensions but the last counted through in order) at most 20 rows name the same one
- gates: bfloat16 [8, 2, 4096, 2], P('pipe', None, 'expert'), may hold values from 0.19921875 to 1
Outputs:
- next_fwd: bfloat16 [8, 4096, 3584], P('pipe', 'expert')
- next_rev: bfloat16 [8, 4096, 3584], P('pipe', 'expert')
The draws below stay inside these ranges and needn't reach their ends.
Inputs may be any that keep to these rules, and one draw needn't show every extreme that they name: `routes`: each row names 2 different experts; among the 128 rows of one device for one section and direction no expert is named more than 20 times, a bound that some block reaches.
All inputs are finite; a program needn't handle non-finite values.
Results may differ from the reference program's by a relative error of at most 0.012.
Values may be sent and summed in bfloat16 or wider, within the bound.
A program may use at most 128 MiB of HBM per device.

```python
import math
import jax
import jax.numpy as jnp
import numpy as np
from jax import lax

D = 3584
FF = 1024
SPLIT = 2
TOPK = 2
TOK_DEV = 128
HID = 512
EXPERTS = 16
CAP = 20
TOKENS = 4096
N_PIPE = 8
N_EXPERT = 32


def levels(rng, dims, cuts, low, high):
    factor_of = 1.0
    for axis_at, blocks in cuts:
        steps = jax.random.uniform(jax.random.fold_in(jax.random.fold_in(rng, 6), axis_at), (blocks,), jnp.float32, low / len(cuts), high / len(cuts))
        factor_of = factor_of * jnp.repeat(jnp.exp(steps), dims[axis_at] // blocks).reshape((-1,) + (1,) * (len(dims) - 1 - axis_at))
    return factor_of


def assign_block(own_key, own, number, rows, count, top, most, slope):
    order = jax.random.permutation(own_key, count)
    crowded, common = load_shares(count, rows * top, most, slope, True), load_shares(count, rows * top, most, slope, False)
    places = jnp.arange(count)

    def named(tallies, turn):
        used = int((tallies > 0).sum())
        fixed = max(1, used // 4)
        moved = fixed + (places - fixed + turn * (used - fixed)) % max(1, count - fixed)
        return jnp.zeros((count,), jnp.int32).at[order[jnp.where(places < fixed, places, moved)]].set(jnp.asarray(tallies, jnp.int32))

    tallies = jnp.where(number % 4 == 0, named(crowded, number // 4), named(common, number - number // 4 - 1))
    mixed = jax.random.permutation(jax.random.fold_in(own, 3), count)
    source_of, receiver = mixed[0:count // 2 * 2:2], mixed[1:count // 2 * 2:2]
    margin = jnp.minimum(tallies[source_of] - 1, most - tallies[receiver]) // 2
    margin = jnp.where((source_of == order[0]) | (receiver == order[0]) | (tallies[receiver] == 0), 0, jnp.maximum(margin, 0))
    moved = jax.random.randint(jax.random.fold_in(own, 4), (count // 2,), 0, 1 << 20) % (margin + 1)
    tallies = tallies.at[source_of].add(-moved).at[receiver].add(moved)
    members = jnp.searchsorted(jnp.cumsum(tallies), jnp.arange(rows * top), side="right").astype(jnp.int32)
    listing = members.reshape(top, rows).T
    listing = listing[jax.random.permutation(jax.random.fold_in(own, 1), rows)]
    turn = jax.random.randint(jax.random.fold_in(own, 2), (rows, 1), 0, top)
    return jnp.take_along_axis(listing, (jnp.arange(top)[None, :] + turn) % top, axis=1)


def load_shares(count, total, most, slope, full):
    loads = [(1 << 20) // math.isqrt(standing ** slope) + 1 for standing in range(1, count + 1)]
    largest = most if full else min(most, max(-(-total // count), total * loads[0] // sum(loads)))
    least = 1 if total - largest >= count - 1 else 0
    given, rest = [largest] + [least] * (count - 1), total - largest - least * (count - 1)
    while rest > 0:
        movable = [i for i in range(1, count) if given[i] < largest] or [i for i in range(1, count) if given[i] < most]
        mass, remaining = sum([loads[i] for i in movable]), rest
        for i in movable:
            addition = min(most - given[i], max(1, remaining * loads[i] // mass), rest)
            given[i] = given[i] + addition
            rest = rest - addition
    return np.array(given)


def normal_values(key, extent, width, most, shards=(), held_as=jnp.bfloat16):
    level = levels(key, extent, shards, -0.22, 0.18) if shards else 1.0
    entries = jax.random.normal(key, extent, jnp.float32) * width * level
    return jnp.minimum(jnp.maximum(entries, -most), most).astype(held_as)


def setup_inputs(seed: int = 0) -> dict:
    key_list = jax.random.split(jax.random.key(seed), 8)
    stream_fwd = normal_values(key_list[0], (N_PIPE, TOKENS, D), 1.0, 6.0, ((0, 8), (1, 32)))
    stream_rev = normal_values(key_list[1], (N_PIPE, TOKENS, D), 1.0, 6.0, ((0, 8), (1, 32)))
    norm_gain = jnp.clip(1.0 + 0.18 * jax.random.normal(key_list[2], (N_PIPE, D), jnp.float32), 0.099609375, 1.8984375).astype(jnp.bfloat16)
    w_up = normal_values(key_list[3], (N_PIPE, N_EXPERT, D, HID), D ** -0.5, 0.09375, ((0, 8), (1, 32)))
    w_down = normal_values(key_list[4], (N_PIPE, N_EXPERT, HID, D), FF ** -0.5, 0.1875, ((0, 8), (1, 32)))
    routes_keys = jax.random.split(jax.random.fold_in(key_list[5], 1), N_PIPE * 2 * TOKENS // TOK_DEV)
    routes_turns = jax.random.permutation(jax.random.fold_in(key_list[5], 3), N_PIPE * 2 * TOKENS // TOK_DEV)
    routes = jax.vmap(lambda own, number: assign_block(jax.random.fold_in(key_list[5], 2), own, number, TOK_DEV, EXPERTS, TOPK, CAP, 1))(routes_keys, routes_turns).reshape((N_PIPE, 2, TOKENS, TOPK))
    gates = jnp.clip(0.19921875 + 0.80078125 * jax.random.uniform(key_list[6], (N_PIPE, 2, TOKENS, TOPK), jnp.float32) ** levels(key_list[6], (N_PIPE, 2, TOKENS, TOPK), ((0, 8), (2, 32)), -0.2, 0.2), 0.19921875, 1.0).astype(jnp.bfloat16)
    return {"stream_fwd": stream_fwd, "stream_rev": stream_rev, "norm_gain": norm_gain, "w_up": w_up, "w_down": w_down, "routes": routes, "gates": gates}


def moe_layer(x, gain, up, down, idx, gval):
    experts = N_EXPERT // SPLIT
    xf = x.astype(jnp.float32)
    scale = lax.rsqrt(lax.optimization_barrier(jnp.mean(xf * xf, axis=-1, keepdims=True)) + 1e-06)
    normed = (xf * scale * gain.astype(jnp.float32)).astype(jnp.bfloat16)
    picks = idx.reshape(N_EXPERT, TOK_DEV * TOPK).astype(jnp.int32)
    match = picks[:, :, None] == jnp.arange(experts, dtype=jnp.int32)[None, None, :]
    ranks = jnp.cumsum(match.astype(jnp.int32), axis=1) - 1
    slots = lax.optimization_barrier(jnp.sum(jnp.where(match, ranks, 0), axis=-1)).astype(jnp.int32)
    source = jnp.broadcast_to(jnp.arange(N_EXPERT, dtype=jnp.int32)[:, None], picks.shape)
    owner = source * TOK_DEV + (jnp.arange(TOK_DEV * TOPK, dtype=jnp.int32) // TOPK)[None, :]
    table = jnp.full((experts, N_EXPERT, CAP), TOKENS, jnp.int32).at[picks, source, slots].set(owner)
    padded = jnp.concatenate([normed, jnp.zeros((1, D), jnp.bfloat16)], axis=0)
    rows = padded[table].reshape(experts, N_EXPERT * CAP, D).astype(jnp.float32)
    upper = up.reshape(experts, SPLIT, D, HID).astype(jnp.float32)
    lower = down.reshape(experts, SPLIT, HID, D).astype(jnp.float32)
    hidden = jax.nn.silu(jnp.einsum('erd,ejdh->ejrh', rows, upper)).astype(jnp.bfloat16)
    partial_value = jnp.einsum('ejrh,ejhd->ejrd', hidden.astype(jnp.float32), lower).astype(jnp.bfloat16)
    expert_out = lax.optimization_barrier(jnp.sum(partial_value.astype(jnp.float32), axis=1)).astype(jnp.bfloat16)
    picked = expert_out[picks, source * CAP + slots]
    picked = picked.reshape(TOKENS, TOPK, D).astype(jnp.float32)
    mixed = xf + lax.optimization_barrier(jnp.sum(gval.astype(jnp.float32)[:, :, None] * picked, axis=1))
    return mixed.astype(jnp.bfloat16)

def reference(stream_fwd, stream_rev, norm_gain, w_up, w_down, routes, gates):
    forward_out = []
    reverse_out = []
    for section in range(N_PIPE):
        forward_out.append(moe_layer(stream_fwd[section], norm_gain[section], w_up[section], w_down[section], routes[section, 0], gates[section, 0]))
        reverse_out.append(moe_layer(stream_rev[section], norm_gain[section], w_up[section], w_down[section], routes[section, 1], gates[section, 1]))
    next_fwd = jnp.roll(jnp.stack(forward_out), 1, axis=0)
    next_rev = jnp.roll(jnp.stack(reverse_out), -1, axis=0)
    return (next_fwd, next_rev)
```

```python
import functools

import jax
import jax.numpy as jnp
from jax import lax
from jax.experimental import pallas as pl
from jax.experimental.pallas import tpu as pltpu
from jax.sharding import PartitionSpec as P

SPLIT = 2
TOPK = 2
NY = 4
NZ = 8
GROUP = 4
MESH = pl.DeviceIdType.MESH

POS = {0: 0, -1: 1, 1: 2, 2: 3, -2: 4, -3: 5, 3: 6, 4: 7}
LEFT, RIGHT = 0, 1


def tile_of(width, most=512):
    tile = 128
    for t in range(128, most + 1, 128):
        if width % t == 0:
            tile = t
    return tile


def kernel(
    cap,
    xf_hbm, xr_hbm, gain_ref, up_hbm, down_hbm, info_ref,
    outf_ref, outr_ref,
    ag, inc, sel, ret, relay, infos, xs, stage, up, down, act, hid, gmat,
    ag_send, ag_recv, inf_send, inf_recv, yd_send, yd_recv, yr_send, yr_recv,
    rs_send, rs_recv, sh_send, sh_recv, load_sem, credit,
):
    tok, width = xs.shape[1], xs.shape[2]
    half = width // 2
    quarter = width // 4
    rows = GROUP * cap
    p = lax.axis_index("pipe")
    e = lax.axis_index("expert")
    n_pipe = lax.axis_size("pipe")
    y, z = e // NZ, e % NZ
    m = z // SPLIT
    zdev = {RIGHT: (p, y * NZ + (z + 1) % NZ), LEFT: (p, y * NZ + (z + NZ - 1) % NZ)}
    ydev = {RIGHT: (p, ((y + 1) % NY) * NZ + z), LEFT: (p, ((y + NY - 1) % NY) * NZ + z)}
    pdev = {0: ((p + 1) % n_pipe, e), 1: ((p + n_pipe - 1) % n_pipe, e)}
    outs = {0: outf_ref, 1: outr_ref}

    def remote(src, dst, send, recv, device):
        return pltpu.make_async_remote_copy(
            src_ref=src, dst_ref=dst, send_sem=send, recv_sem=recv,
            device_id=device, device_id_type=MESH,
        )

    barrier = pltpu.get_barrier_semaphore()
    for device in (zdev[0], zdev[1], ydev[0], ydev[1], pdev[0], pdev[1]):
        pl.semaphore_signal(barrier, inc=1, device_id=device, device_id_type=MESH)

    loads = [
        pltpu.make_async_copy(xf_hbm, xs.at[0], load_sem.at[0]),
        pltpu.make_async_copy(xr_hbm, xs.at[1], load_sem.at[1]),
        pltpu.make_async_copy(up_hbm, up, load_sem.at[2]),
        pltpu.make_async_copy(down_hbm, down, load_sem.at[3]),
    ]
    for load in loads:
        load.start()

    def normalise(s):
        gain = gain_ref[...].astype(jnp.float32)

        def body(i, carry):
            at = pl.ds(pl.multiple_of(i * 16, 16), 16)
            x = xs[s, at, :].astype(jnp.float32)
            scale = lax.rsqrt(jnp.mean(x * x, axis=-1, keepdims=True) + 1e-06)
            ag[s, 0, at, :] = (x * scale * gain).astype(jnp.bfloat16)
            return carry

        lax.fori_loop(0, tok // 16, body, 0)

    def ag_copy(s, way, hop, c):
        sign = -1 if way == RIGHT else 1
        source, target = sign * (hop - 1), sign * hop
        source, target = POS[source], POS[4 if abs(target) == 4 else target]
        cols = pl.ds(c * half, half)
        return remote(
            ag.at[s, source, :, cols], ag.at[s, target, :, cols],
            ag_send.at[s, way, hop - 1, c], ag_recv.at[s, way, hop - 1, c], zdev[way],
        )

    def inf_copy(way, hop):
        sign = -1 if way == RIGHT else 1
        source, target = sign * (hop - 1), sign * hop
        source, target = POS[source], POS[4 if abs(target) == 4 else target]
        return remote(
            infos.at[source], infos.at[target],
            inf_send.at[way, hop - 1], inf_recv.at[way, hop - 1], zdev[way],
        )

    def ag_parts(way, hop):
        if hop < 4:
            return (0, 1)
        return (0,) if way == RIGHT else (1,)

    def inf_ways(hop):
        return (RIGHT, LEFT) if hop < 4 else (RIGHT,)

    def gather_hop(s, hop):
        if s == 0:
            for way in inf_ways(hop):
                if hop > 1:
                    inf_copy(way, hop - 1).wait_recv()
                inf_copy(way, hop).start()
        for c in (0, 1):
            for way in (RIGHT, LEFT):
                if hop > 1:
                    ag_copy(s, way, hop - 1, c).wait_recv()
                if c in ag_parts(way, hop):
                    ag_copy(s, way, hop, c).start()

    def gather_end(s):
        if s == 0:
            inf_copy(RIGHT, 4).wait_recv()
            inf_copy(LEFT, 3).wait_recv()
            for hop in (1, 2, 3, 4):
                for way in inf_ways(hop):
                    inf_copy(way, hop).wait_send()
        for way in (RIGHT, LEFT):
            for c in ag_parts(way, 4):
                ag_copy(s, way, 4, c).wait_recv()

    def gather_sent(s):
        for hop in (1, 2, 3, 4):
            for way in (RIGHT, LEFT):
                for c in ag_parts(way, hop):
                    ag_copy(s, way, hop, c).wait_send()

    def row_codes(shape):
        r = lax.broadcasted_iota(jnp.int32, shape, 0)
        one, zero = jnp.int32(1), jnp.int32(0)
        d = sum(jnp.where(r >= k * rows, one, zero) for k in (1, 2, 3))
        r = r - d * rows
        i = sum(jnp.where(r >= k * cap, one, zero) for k in (1, 2, 3))
        c = r - i * cap
        yd = y + d
        yd = yd - jnp.where(yd >= NY, NY * one, zero)
        expert = yd * (NZ // SPLIT) + m
        return ((i * NY * (NZ // SPLIT) + expert) * cap + c).astype(jnp.float32)

    per_source = NY * (NZ // SPLIT) * cap

    def select(s, g):
        codes = row_codes((NY * rows, tok))
        parts = []
        for i in range(GROUP):
            info = infos[GROUP * g + i]
            hit0 = codes == info[4 * s : 4 * s + 1, :] + float(i * per_source)
            hit1 = codes == info[4 * s + 1 : 4 * s + 2, :] + float(i * per_source)
            parts.append(jnp.where(hit0 | hit1, 1.0, 0.0).astype(jnp.bfloat16))
            weights = jnp.where(hit0, info[4 * s + 2 : 4 * s + 3, :], 0.0) + jnp.where(
                hit1, info[4 * s + 3 : 4 * s + 4, :], 0.0
            )
            gmat[s, GROUP * g + i] = weights.T.astype(jnp.bfloat16)
        pick = jnp.concatenate(parts, axis=1)
        tile = tile_of(width)

        def body(j, carry):
            cols = pl.ds(pl.multiple_of(j * tile, 128), tile)
            block = ag[s, GROUP * g : GROUP * (g + 1), :, cols].reshape(GROUP * tok, tile)
            out = jnp.dot(pick, block, preferred_element_type=jnp.float32).astype(jnp.bfloat16)
            inc[s, g, 0:rows, cols] = out[0:rows]
            sel[s, g, :, cols] = out[rows:]
            return carry

        lax.fori_loop(0, width // tile, body, 0)

    low, high = pl.ds(0, half), pl.ds(half, half)

    def at(d):
        return pl.ds(d * rows, rows)

    def yd_copies(s, g):
        ss, rr = yd_send.at[s, g], yd_recv.at[s, g]
        source, into, hop = sel.at[s, g], inc.at[s, g], relay.at[s, g, 0]
        first = [
            remote(source.at[at(1), low], hop.at[0], ss.at[0], rr.at[0], ydev[RIGHT]),
            remote(source.at[at(1), high], hop.at[1], ss.at[1], rr.at[1], ydev[LEFT]),
        ]
        direct = [
            remote(source.at[at(0)], into.at[at(1)], ss.at[2], rr.at[2], ydev[RIGHT]),
            remote(source.at[at(2)], into.at[at(3)], ss.at[3], rr.at[3], ydev[LEFT]),
        ]
        second = [
            remote(hop.at[0], into.at[at(2), low], ss.at[4], rr.at[4], ydev[RIGHT]),
            remote(hop.at[1], into.at[at(2), high], ss.at[5], rr.at[5], ydev[LEFT]),
        ]
        return first, direct, second

    def yr_copies(s, g):
        ss, rr = yr_send.at[s, g], yr_recv.at[s, g]
        source, into, hop = inc.at[s, g], ret.at[s, g], relay.at[s, g, 1]
        first = [
            remote(source.at[at(2), low], hop.at[0], ss.at[0], rr.at[0], ydev[LEFT]),
            remote(source.at[at(2), high], hop.at[1], ss.at[1], rr.at[1], ydev[RIGHT]),
        ]
        direct = [
            remote(source.at[at(1)], into.at[at(1)], ss.at[2], rr.at[2], ydev[LEFT]),
            remote(source.at[at(3)], into.at[at(3)], ss.at[3], rr.at[3], ydev[RIGHT]),
        ]
        second = [
            remote(hop.at[0], into.at[at(2), low], ss.at[4], rr.at[4], ydev[LEFT]),
            remote(hop.at[1], into.at[at(2), high], ss.at[5], rr.at[5], ydev[RIGHT]),
        ]
        return first, direct, second

    def y_start(copies):
        first, direct, _ = copies
        for copy in first + direct:
            copy.start()

    def y_relay(copies):
        first, _, second = copies
        for a, b in zip(first, second):
            a.wait_recv()
            b.start()

    def y_wait(copies):
        _, direct, second = copies
        for copy in direct + second:
            copy.wait_recv()

    def y_sent(copies):
        for part in copies:
            for copy in part:
                copy.wait_send()

    def experts(s, g):
        tile = tile_of(width)
        hid[...] = jnp.zeros_like(hid)

        def upper(j, carry):
            cols = pl.ds(pl.multiple_of(j * tile, 128), tile)
            hid[...] += jnp.dot(inc[s, g, :, cols], up[cols, :], preferred_element_type=jnp.float32)
            return carry

        lax.fori_loop(0, width // tile, upper, 0)
        act[...] = jax.nn.silu(hid[...]).astype(jnp.bfloat16)

        def lower(j, carry):
            cols = pl.ds(pl.multiple_of(j * tile, 128), tile)
            out = jnp.dot(act[...], down[:, cols], preferred_element_type=jnp.float32)
            out = out.astype(jnp.bfloat16)
            ret[s, g, 0:rows, cols] = out[0:rows]
            inc[s, g, rows:, cols] = out[rows:]
            return carry

        lax.fori_loop(0, width // tile, lower, 0)

    def rs_copy(s, way, step, c):
        cols = pl.ds(pl.multiple_of(c * quarter, 128), quarter)
        if step == 0:
            source = stage.at[s, :, cols]
        else:
            source = ag.at[s, 4 * way + step - 1, :, cols]
        return remote(
            source, ag.at[s, 4 * way + step, :, cols],
            rs_send.at[s, way, step, c], rs_recv.at[s, way, step, c], zdev[way],
        )

    def share(s, pos, c):
        cols = pl.ds(pl.multiple_of(c * quarter, 128), quarter)
        return jnp.dot(
            gmat[s, pos], ret[s, pos // GROUP, :, cols], preferred_element_type=jnp.float32
        )

    def rs_pos(way, step):
        away = 4 - step
        if away == 4:
            return POS[4]
        return POS[-away if way == LEFT else away]

    def rs_begin(s):
        def body(j, carry):
            for way, c in ((LEFT, j), (RIGHT, j + 2)):
                cols = pl.ds(pl.multiple_of(c * quarter, 128), quarter)
                stage[s, :, cols] = share(s, rs_pos(way, 0), c).astype(jnp.bfloat16)
                rs_copy(s, way, 0, c).start()
            return carry

        lax.fori_loop(0, 2, body, 0)

        def fresh(j, carry):
            for way, c in ((LEFT, j + 2), (RIGHT, j)):
                cols = pl.ds(pl.multiple_of(c * quarter, 128), quarter)
                ag[s, 4 * way, :, cols] = share(s, rs_pos(way, 1), c).astype(jnp.bfloat16)
                rs_copy(s, way, 1, c).start()
            return carry

        lax.fori_loop(0, 2, fresh, 0)

    def rs_add(s, way, step, c):
        cols = pl.ds(pl.multiple_of(c * quarter, 128), quarter)
        own = share(s, rs_pos(way, step), c)
        rs_copy(s, way, step - 1, c).wait_recv()
        total = own + ag[s, 4 * way + step - 1, :, cols].astype(jnp.float32)
        ag[s, 4 * way + step - 1, :, cols] = total.astype(jnp.bfloat16)
        rs_copy(s, way, step, c).start()

    def rs_step(s, step):
        def body(j, carry):
            rs_add(s, LEFT, step, (j + 2) % 4 if step > 1 else j)
            rs_add(s, RIGHT, step, j if step > 1 else j + 2)
            return carry

        lax.fori_loop(0, 4 if step > 1 else 2, body, 0)

    def sh_copy(s, c):
        cols = pl.ds(pl.multiple_of(c * quarter, 128), quarter)
        return remote(
            stage.at[s, :, cols], outs[s].at[:, cols], sh_send.at[s, c], sh_recv.at[s, c], pdev[s]
        )

    def rs_end(s):
        def sent(j, carry):
            rs_copy(s, LEFT, 0, j).wait_send()
            rs_copy(s, RIGHT, 0, j + 2).wait_send()
            return carry

        lax.fori_loop(0, 2, sent, 0)

        def body(j, carry):
            c = (j + 2) % 4
            cols = pl.ds(pl.multiple_of(c * quarter, 128), quarter)
            own = share(s, POS[0], c) + xs[s, :, cols].astype(jnp.float32)
            rs_copy(s, LEFT, 3, c).wait_recv()
            rs_copy(s, RIGHT, 3, c).wait_recv()
            total = own + (
                ag[s, 3, :, cols].astype(jnp.float32) + ag[s, 7, :, cols].astype(jnp.float32)
            )
            stage[s, :, cols] = total.astype(jnp.bfloat16)
            sh_copy(s, c).start()
            return carry

        lax.fori_loop(0, 4, body, 0)

    def rs_sent(s):
        def body(c, carry):
            for way in (LEFT, RIGHT):
                for step in (1, 2, 3):
                    rs_copy(s, way, step, c).wait_send()
            sh_copy(s, c).wait()
            return carry

        lax.fori_loop(0, 4, body, 0)

    def give_credit(s):
        gather_sent(s)
        for way in (LEFT, RIGHT):
            pl.semaphore_signal(credit.at[s], inc=1, device_id=zdev[way], device_id_type=MESH)

    infos[0] = info_ref[...]
    loads[0].wait()
    normalise(0)
    pl.semaphore_wait(barrier, 6)

    gather_hop(0, 1)
    loads[1].wait()
    normalise(1)
    gather_hop(0, 2)
    gather_hop(0, 3)
    select(0, 0)
    y_start(yd_copies(0, 0))
    y_relay(yd_copies(0, 0))
    gather_hop(0, 4)
    gather_hop(1, 1)
    loads[2].wait()
    loads[3].wait()
    y_wait(yd_copies(0, 0))
    experts(0, 0)
    y_start(yr_copies(0, 0))
    gather_end(0)
    select(0, 1)
    y_start(yd_copies(0, 1))
    y_relay(yr_copies(0, 0))
    gather_hop(1, 2)
    give_credit(0)
    y_relay(yd_copies(0, 1))
    y_wait(yd_copies(0, 1))
    experts(0, 1)
    y_start(yr_copies(0, 1))
    gather_hop(1, 3)
    select(1, 0)
    y_start(yd_copies(1, 0))
    y_relay(yr_copies(0, 1))
    y_relay(yd_copies(1, 0))
    y_wait(yr_copies(0, 0))
    y_wait(yr_copies(0, 1))
    gather_hop(1, 4)
    pl.semaphore_wait(credit.at[0], 2)
    rs_begin(0)
    y_wait(yd_copies(1, 0))
    experts(1, 0)
    y_start(yr_copies(1, 0))
    gather_end(1)
    select(1, 1)
    y_start(yd_copies(1, 1))
    rs_step(0, 1)
    give_credit(1)
    y_relay(yr_copies(1, 0))
    y_relay(yd_copies(1, 1))
    rs_step(0, 2)
    y_wait(yd_copies(1, 1))
    experts(1, 1)
    y_start(yr_copies(1, 1))
    rs_step(0, 3)
    y_relay(yr_copies(1, 1))
    y_wait(yr_copies(1, 0))
    y_wait(yr_copies(1, 1))
    pl.semaphore_wait(credit.at[1], 2)
    rs_begin(1)
    rs_end(0)
    rs_step(1, 1)
    rs_step(1, 2)
    rs_step(1, 3)
    rs_end(1)
    for s in (0, 1):
        for g in (0, 1):
            y_sent(yd_copies(s, g))
            y_sent(yr_copies(s, g))
        rs_sent(s)


def shards(stream_fwd, stream_rev, norm_gain, w_up, w_down, routes, gates):
    xf, xr = stream_fwd[0], stream_rev[0]
    upper, lower = w_up[0, 0], w_down[0, 0]
    tok, width = xf.shape
    hidden = upper.shape[1]
    experts = lax.axis_size("expert") // SPLIT
    cap = SPLIT * max(1, tok * TOPK * 5 // (4 * SPLIT * experts))
    picks = routes[0].reshape(2, tok * TOPK)
    match = (picks[:, :, None] == jnp.arange(experts, dtype=jnp.int32)).astype(jnp.bfloat16)
    earlier = jnp.tri(tok * TOPK, k=-1, dtype=jnp.bfloat16)
    before = jnp.einsum("uv,sve->sue", earlier, match, preferred_element_type=jnp.float32)
    slots = jnp.sum(before * match.astype(jnp.float32), axis=-1)
    target = picks.astype(jnp.float32) * cap + slots
    info = jnp.concatenate(
        [
            target.reshape(2, tok, TOPK).transpose(0, 2, 1),
            gates[0].astype(jnp.float32).transpose(0, 2, 1),
        ],
        axis=1,
    ).reshape(8, tok)
    rows = GROUP * cap
    bf16 = jnp.bfloat16
    dma = pltpu.SemaphoreType.DMA
    anywhere = pl.BlockSpec(memory_space=pl.ANY)
    in_vmem = pl.BlockSpec(memory_space=pltpu.VMEM)
    outf, outr = pl.pallas_call(
        functools.partial(kernel, cap),
        out_shape=(jax.ShapeDtypeStruct((tok, width), bf16),) * 2,
        in_specs=[anywhere, anywhere, in_vmem, anywhere, anywhere, in_vmem],
        out_specs=(anywhere, anywhere),
        scratch_shapes=[
            pltpu.VMEM((2, NZ, tok, width), bf16),
            pltpu.VMEM((2, 2, NY * rows, width), bf16),
            pltpu.VMEM((2, 2, (NY - 1) * rows, width), bf16),
            pltpu.VMEM((2, 2, NY * rows, width), bf16),
            pltpu.VMEM((2, 2, 2, 2, rows, width // 2), bf16),
            pltpu.VMEM((NZ, 8, tok), jnp.float32),
            pltpu.VMEM((2, tok, width), bf16),
            pltpu.VMEM((2, tok, width), bf16),
            pltpu.VMEM((width, hidden), bf16),
            pltpu.VMEM((hidden, width), bf16),
            pltpu.VMEM((NY * rows, hidden), bf16),
            pltpu.VMEM((NY * rows, hidden), jnp.float32),
            pltpu.VMEM((2, NZ, tok, NY * rows), bf16),
            dma((2, 2, 4, 2)), dma((2, 2, 4, 2)),
            dma((2, 4)), dma((2, 4)),
            dma((2, 2, 6)), dma((2, 2, 6)),
            dma((2, 2, 6)), dma((2, 2, 6)),
            dma((2, 2, 4, 4)), dma((2, 2, 4, 4)),
            dma((2, 4)), dma((2, 4)),
            dma((4,)),
            pltpu.SemaphoreType.REGULAR((2,)),
        ],
        compiler_params=pltpu.CompilerParams(
            collective_id=0, has_side_effects=True, vmem_limit_bytes=62 * 1024 * 1024
        ),
        cost_estimate=pl.CostEstimate(
            flops=2 * 2 * 2 * NZ * NY * cap * width * hidden,
            bytes_accessed=16 * 1024 * 1024,
            transcendentals=0,
        ),
    )(xf, xr, norm_gain, upper, lower, info)
    return outf[None], outr[None]


def solution(mesh):
    return jax.shard_map(
        shards,
        mesh=mesh,
        in_specs=(
            P("pipe", "expert", None),
            P("pipe", "expert", None),
            P("pipe", None),
            P("pipe", "expert", None, None),
            P("pipe", "expert", None, None),
            P("pipe", None, "expert", None),
            P("pipe", None, "expert", None),
        ),
        out_specs=(P("pipe", "expert", None), P("pipe", "expert", None)),
        check_vma=False,
    )
```

```python
import functools

import jax
import jax.numpy as jnp
from jax import lax
from jax.experimental import pallas as pl
from jax.experimental.pallas import tpu as pltpu
from jax.sharding import PartitionSpec as P

SPLIT = 2
TOPK = 2
NY = 4
NZ = 8
GROUP = 4
MESH = pl.DeviceIdType.MESH

POS = {0: 0, -1: 1, 1: 2, 2: 3, -2: 4, -3: 5, 3: 6, 4: 7}
LEFT, RIGHT = 0, 1


def tile_of(width, most=512):
    tile = 128
    for t in range(128, most + 1, 128):
        if width % t == 0:
            tile = t
    return tile


def kernel(
    cap,
    xf_hbm, xr_hbm, gain_ref, up_hbm, down_hbm, info_ref,
    outf_ref, outr_ref,
    ag, inc, sel, ret, infos, xs, stage, up, down, act, hid, gmat,
    ag_send, ag_recv, inf_send, inf_recv, yd_send, yd_recv, yr_send, yr_recv,
    rs_send, rs_recv, sh_send, sh_recv, load_sem, credit,
):
    tok, width = xs.shape[1], xs.shape[2]
    half = width // 2
    quarter = width // 4
    rows = GROUP * cap
    experts = NY * (NZ // SPLIT)
    p = lax.axis_index("pipe")
    e = lax.axis_index("expert")
    n_pipe = lax.axis_size("pipe")
    y, z = e // NZ, e % NZ
    m = z // SPLIT
    zdev = {RIGHT: (p, y * NZ + (z + 1) % NZ), LEFT: (p, y * NZ + (z + NZ - 1) % NZ)}
    ydev = {d: (p, ((y + d) % NY) * NZ + z) for d in (1, 2, 3)}
    pdev = {0: ((p + 1) % n_pipe, e), 1: ((p + n_pipe - 1) % n_pipe, e)}
    outs = {0: outf_ref, 1: outr_ref}

    def remote(src, dst, send, recv, device):
        return pltpu.make_async_remote_copy(
            src_ref=src, dst_ref=dst, send_sem=send, recv_sem=recv,
            device_id=device, device_id_type=MESH,
        )

    barrier = pltpu.get_barrier_semaphore()
    peers = [zdev[0], zdev[1], ydev[1], ydev[2], ydev[3], pdev[0], pdev[1]]
    for device in peers:
        pl.semaphore_signal(barrier, inc=1, device_id=device, device_id_type=MESH)

    load_xf = pltpu.make_async_copy(xf_hbm, xs.at[0], load_sem.at[0])
    load_xr = pltpu.make_async_copy(xr_hbm, xs.at[1], load_sem.at[1])
    load_up = pltpu.make_async_copy(up_hbm, up, load_sem.at[2])
    load_down = pltpu.make_async_copy(down_hbm, down, load_sem.at[3])

    def normalise(s):
        gain = gain_ref[...].astype(jnp.float32)

        def body(i, carry):
            at = pl.ds(pl.multiple_of(i * 16, 16), 16)
            x = xs[s, at, :].astype(jnp.float32)
            scale = lax.rsqrt(jnp.mean(x * x, axis=-1, keepdims=True) + 1e-06)
            ag[s, 0, at, :] = (x * scale * gain).astype(jnp.bfloat16)
            return carry

        lax.fori_loop(0, tok // 16, body, 0)

    def own_info():
        here = lax.broadcasted_iota(jnp.int32, (experts, tok), 0).astype(jnp.float32)
        t0 = lax.broadcasted_iota(jnp.int32, (tok, tok), 0)
        t1 = lax.broadcasted_iota(jnp.int32, (tok, tok), 1)
        earlier = jnp.where(t0 < t1, 1.0, 0.0).astype(jnp.bfloat16)
        for s in (0, 1):
            hits = [here == info_ref[4 * s + k : 4 * s + k + 1, :] for k in range(TOPK)]
            named = jnp.where(hits[0] | hits[1], 1.0, 0.0).astype(jnp.bfloat16)
            before = jnp.dot(named, earlier, preferred_element_type=jnp.float32)
            for k in range(TOPK):
                code = jnp.where(hits[k], here * cap + before, 0.0)
                infos[0, 4 * s + k : 4 * s + k + 1, :] = jnp.sum(code, axis=0, keepdims=True)
            infos[0, 4 * s + 2 : 4 * s + 4, :] = info_ref[4 * s + 2 : 4 * s + 4, :]

    def pos_of(delta):
        return POS[4 if abs(delta) == 4 else delta]

    def ag_copy(s, way, hop, c):
        sign = -1 if way == RIGHT else 1
        cols = pl.ds(c * quarter, quarter)
        return remote(
            ag.at[s, pos_of(sign * (hop - 1)), :, cols], ag.at[s, pos_of(sign * hop), :, cols],
            ag_send.at[s, way, hop - 1, c], ag_recv.at[s, way, hop - 1, c], zdev[way],
        )

    def inf_copy(way, hop):
        sign = -1 if way == RIGHT else 1
        return remote(
            infos.at[pos_of(sign * (hop - 1))], infos.at[pos_of(sign * hop)],
            inf_send.at[way, hop - 1], inf_recv.at[way, hop - 1], zdev[way],
        )

    def inf_ways(hop):
        return (RIGHT, LEFT) if hop < 4 else (RIGHT,)

    def inf_hop(hop):
        for way in inf_ways(hop):
            if hop > 1:
                inf_copy(way, hop - 1).wait_recv()
            inf_copy(way, hop).start()

    def first_chunk(way, h):
        return 2 * h if way == RIGHT else 2 * h + 1

    def gather_hop(s, h, hop):
        for turn in (0, 1):
            for way in (RIGHT, LEFT):
                c = first_chunk(way, h) ^ turn
                if hop > 1:
                    ag_copy(s, way, hop - 1, c).wait_recv()
                ag_copy(s, way, hop, c).start()

    def gather_last(s, h):
        for way in (RIGHT, LEFT):
            c = first_chunk(way, h)
            ag_copy(s, way, 3, c).wait_recv()
            ag_copy(s, way, 4, c).start()

    def gather_end(s, h):
        for way in (RIGHT, LEFT):
            ag_copy(s, way, 3, first_chunk(way, h) ^ 1).wait_recv()
        for way in (RIGHT, LEFT):
            ag_copy(s, way, 4, first_chunk(way, h)).wait_recv()

    def gather_sent(s):
        for h in (0, 1):
            for way in (RIGHT, LEFT):
                for hop in (1, 2, 3):
                    for c in (2 * h, 2 * h + 1):
                        ag_copy(s, way, hop, c).wait_send()
                ag_copy(s, way, 4, first_chunk(way, h)).wait_send()

    def row_codes(shape):
        r = lax.broadcasted_iota(jnp.int32, shape, 0)
        one, zero = jnp.int32(1), jnp.int32(0)
        d = sum(jnp.where(r >= k * rows, one, zero) for k in (1, 2, 3))
        r = r - d * rows
        i = sum(jnp.where(r >= k * cap, one, zero) for k in (1, 2, 3))
        c = r - i * cap
        yd = y + d
        yd = yd - jnp.where(yd >= NY, NY * one, zero)
        expert = yd * (NZ // SPLIT) + m
        return ((i * experts + expert) * cap + c).astype(jnp.float32)

    def select(s, h, g):
        codes = row_codes((NY * rows, tok))
        parts = []
        for i in range(GROUP):
            info = infos[GROUP * g + i]
            shift = float(i * experts * cap)
            hit0 = codes == info[4 * s : 4 * s + 1, :] + shift
            hit1 = codes == info[4 * s + 1 : 4 * s + 2, :] + shift
            parts.append(jnp.where(hit0 | hit1, 1.0, 0.0).astype(jnp.bfloat16))
            if h == 0:
                weights = jnp.where(hit0, info[4 * s + 2 : 4 * s + 3, :], 0.0) + jnp.where(
                    hit1, info[4 * s + 3 : 4 * s + 4, :], 0.0
                )
                gmat[s, GROUP * g + i] = weights.T.astype(jnp.bfloat16)
        pick = jnp.concatenate(parts, axis=1)
        tile = tile_of(half)

        def body(j, carry):
            cols = pl.ds(pl.multiple_of(h * half + j * tile, 128), tile)
            block = ag[s, GROUP * g : GROUP * (g + 1), :, cols].reshape(GROUP * tok, tile)
            out = jnp.dot(pick, block, preferred_element_type=jnp.float32).astype(jnp.bfloat16)
            inc[s, g, 0:rows, cols] = out[0:rows]
            sel[s, g, :, cols] = out[rows:]
            return carry

        lax.fori_loop(0, half // tile, body, 0)
        for d in (1, 2, 3):
            yd_copy(s, h, g, d).start()

    def yd_copy(s, h, g, d):
        cols = pl.ds(h * half, half)
        return remote(
            sel.at[s, g, pl.ds((d - 1) * rows, rows), cols],
            inc.at[s, g, pl.ds(d * rows, rows), cols],
            yd_send.at[s, h, g, d - 1], yd_recv.at[s, h, g, d - 1], ydev[d],
        )

    def yr_copy(s, h, g, d):
        cols = pl.ds(h * half, half)
        block = pl.ds(d * rows, rows)
        return remote(
            inc.at[s, g, block, cols], ret.at[s, g, block, cols],
            yr_send.at[s, h, g, d - 1], yr_recv.at[s, h, g, d - 1], ydev[NY - d],
        )

    def back(s, h, g):
        for d in (1, 2, 3):
            yr_copy(s, h, g, d).wait_recv()

    def upper(s, h, g):
        for d in (1, 2, 3):
            yd_copy(s, h, g, d).wait_recv()
        tile = tile_of(half)
        if h == 0:
            hid[g] = jnp.zeros(hid.shape[1:], jnp.float32)

        def body(j, carry):
            cols = pl.ds(pl.multiple_of(h * half + j * tile, 128), tile)
            hid[g] += jnp.dot(inc[s, g, :, cols], up[cols, :], preferred_element_type=jnp.float32)
            return carry

        lax.fori_loop(0, half // tile, body, 0)
        if h == 1:
            act[g] = jax.nn.silu(hid[g]).astype(jnp.bfloat16)

    def lower(s, h, g):
        tile = tile_of(half)

        def body(j, carry):
            cols = pl.ds(pl.multiple_of(h * half + j * tile, 128), tile)
            out = jnp.dot(act[g], down[:, cols], preferred_element_type=jnp.float32)
            out = out.astype(jnp.bfloat16)
            ret[s, g, 0:rows, cols] = out[0:rows]
            inc[s, g, rows:, cols] = out[rows:]
            return carry

        lax.fori_loop(0, half // tile, body, 0)
        for d in (2, 1, 3):
            yr_copy(s, h, g, d).start()

    def rs_copy(s, way, step, c):
        cols = pl.ds(c * quarter, quarter)
        if step == 0:
            source = stage.at[s, :, cols]
        else:
            source = ag.at[s, 4 * way + step - 1, :, cols]
        return remote(
            source, ag.at[s, 4 * way + step, :, cols],
            rs_send.at[s, way, step, c], rs_recv.at[s, way, step, c], zdev[way],
        )

    def share(s, pos, c):
        cols = pl.ds(c * quarter, quarter)
        return jnp.dot(
            gmat[s, pos], ret[s, pos // GROUP, :, cols], preferred_element_type=jnp.float32
        )

    def rs_pos(way, step):
        away = 4 - step
        if away == 4:
            return POS[4]
        return POS[-away if way == LEFT else away]

    def rs_first(way, h):
        return 2 * h if way == LEFT else 2 * h + 1

    def rs_begin(s, h):
        for way in (LEFT, RIGHT):
            c = rs_first(way, h)
            stage[s, :, pl.ds(c * quarter, quarter)] = share(s, rs_pos(way, 0), c).astype(jnp.bfloat16)
            rs_copy(s, way, 0, c).start()
        for way in (LEFT, RIGHT):
            c = rs_first(way, h) ^ 1
            ag[s, 4 * way, :, pl.ds(c * quarter, quarter)] = share(s, rs_pos(way, 1), c).astype(
                jnp.bfloat16
            )
            rs_copy(s, way, 1, c).start()

    def rs_add(s, way, step, c):
        cols = pl.ds(c * quarter, quarter)
        own = share(s, rs_pos(way, step), c)
        rs_copy(s, way, step - 1, c).wait_recv()
        total = own + ag[s, 4 * way + step - 1, :, cols].astype(jnp.float32)
        ag[s, 4 * way + step - 1, :, cols] = total.astype(jnp.bfloat16)
        rs_copy(s, way, step, c).start()

    def rs_step(s, h, step):
        for turn in (1, 0) if step > 1 else (0,):
            for way in (LEFT, RIGHT):
                rs_add(s, way, step, rs_first(way, h) ^ turn)

    def sh_copy(s, c):
        cols = pl.ds(c * quarter, quarter)
        return remote(
            stage.at[s, :, cols], outs[s].at[:, cols], sh_send.at[s, c], sh_recv.at[s, c], pdev[s]
        )

    def rs_end(s, h):
        for way in (LEFT, RIGHT):
            rs_copy(s, way, 0, rs_first(way, h)).wait_send()
        for c in (2 * h, 2 * h + 1):
            cols = pl.ds(c * quarter, quarter)
            own = share(s, POS[0], c) + xs[s, :, cols].astype(jnp.float32)
            rs_copy(s, LEFT, 3, c).wait_recv()
            rs_copy(s, RIGHT, 3, c).wait_recv()
            total = own + (
                ag[s, 3, :, cols].astype(jnp.float32) + ag[s, 7, :, cols].astype(jnp.float32)
            )
            stage[s, :, cols] = total.astype(jnp.bfloat16)
            sh_copy(s, c).start()

    def finish(s):
        for h in (0, 1):
            for g in (0, 1):
                for d in (1, 2, 3):
                    yd_copy(s, h, g, d).wait_send()
                    yr_copy(s, h, g, d).wait_send()
            for c in (2 * h, 2 * h + 1):
                for way in (LEFT, RIGHT):
                    for step in (1, 2, 3):
                        rs_copy(s, way, step, c).wait_send()
                sh_copy(s, c).wait()

    def give_credit(s):
        gather_sent(s)
        for way in (LEFT, RIGHT):
            pl.semaphore_signal(credit.at[s], inc=1, device_id=zdev[way], device_id_type=MESH)

    f, r, near, far = 0, 1, 0, 1

    load_xf.start()
    load_xr.start()
    own_info()
    load_xf.wait()
    normalise(f)
    pl.semaphore_wait(barrier, len(peers))

    inf_hop(1)
    gather_hop(f, 0, 1)
    load_up.start()
    load_down.start()
    load_xr.wait()
    normalise(r)
    inf_hop(2)
    gather_hop(f, 0, 2)
    inf_hop(3)
    gather_hop(f, 0, 3)
    select(f, 0, near)
    inf_hop(4)
    gather_last(f, 0)
    gather_hop(f, 1, 1)
    load_up.wait()
    load_down.wait()
    inf_copy(RIGHT, 4).wait_recv()
    inf_copy(LEFT, 3).wait_recv()
    gather_end(f, 0)
    select(f, 0, far)
    gather_hop(f, 1, 2)
    upper(f, 0, near)
    gather_hop(f, 1, 3)
    select(f, 1, near)
    upper(f, 0, far)
    gather_last(f, 1)
    gather_hop(r, 0, 1)
    gather_end(f, 1)
    select(f, 1, far)
    gather_hop(r, 0, 2)
    upper(f, 1, near)
    give_credit(f)
    gather_hop(r, 0, 3)
    select(r, 0, near)
    upper(f, 1, far)
    lower(f, 0, far)
    gather_last(r, 0)
    gather_hop(r, 1, 1)
    lower(f, 0, near)
    gather_end(r, 0)
    select(r, 0, far)
    gather_hop(r, 1, 2)
    upper(r, 0, near)
    lower(f, 1, far)
    gather_hop(r, 1, 3)
    select(r, 1, near)
    gather_last(r, 1)
    back(f, 0, far)
    pl.semaphore_wait(credit.at[f], 2)
    rs_begin(f, 0)
    gather_end(r, 1)
    select(r, 1, far)
    back(f, 0, near)
    rs_step(f, 0, 1)
    give_credit(r)
    rs_step(f, 0, 2)
    upper(r, 0, far)
    lower(f, 1, near)
    rs_step(f, 0, 3)
    back(f, 1, far)
    rs_begin(f, 1)
    rs_end(f, 0)
    upper(r, 1, near)
    rs_step(f, 1, 1)
    back(f, 1, near)
    rs_step(f, 1, 2)
    upper(r, 1, far)
    lower(r, 0, far)
    lower(r, 0, near)
    rs_step(f, 1, 3)
    lower(r, 1, far)
    lower(r, 1, near)
    pl.semaphore_wait(credit.at[r], 2)
    back(r, 0, far)
    rs_begin(r, 0)
    rs_end(f, 1)
    rs_step(r, 0, 1)
    back(r, 0, near)
    rs_step(r, 0, 2)
    rs_step(r, 0, 3)
    back(r, 1, far)
    rs_begin(r, 1)
    rs_end(r, 0)
    rs_step(r, 1, 1)
    back(r, 1, near)
    rs_step(r, 1, 2)
    rs_step(r, 1, 3)
    rs_end(r, 1)
    for hop in (1, 2, 3, 4):
        for way in inf_ways(hop):
            inf_copy(way, hop).wait_send()
    finish(f)
    finish(r)


def shards(stream_fwd, stream_rev, norm_gain, w_up, w_down, routes, gates):
    xf, xr = stream_fwd[0], stream_rev[0]
    upper, lower = w_up[0, 0], w_down[0, 0]
    tok, width = xf.shape
    hidden = upper.shape[1]
    experts = lax.axis_size("expert") // SPLIT
    cap = SPLIT * max(1, tok * TOPK * 5 // (4 * SPLIT * experts))
    info = jnp.concatenate([routes[0].astype(jnp.float32), gates[0].astype(jnp.float32)], axis=-1)
    info = info.transpose(0, 2, 1).reshape(8, tok)
    rows = GROUP * cap
    bf16 = jnp.bfloat16
    dma = pltpu.SemaphoreType.DMA
    anywhere = pl.BlockSpec(memory_space=pl.ANY)
    in_vmem = pl.BlockSpec(memory_space=pltpu.VMEM)
    outf, outr = pl.pallas_call(
        functools.partial(kernel, cap),
        out_shape=(jax.ShapeDtypeStruct((tok, width), bf16),) * 2,
        in_specs=[anywhere, anywhere, in_vmem, anywhere, anywhere, in_vmem],
        out_specs=(anywhere, anywhere),
        scratch_shapes=[
            pltpu.VMEM((2, NZ, tok, width), bf16),
            pltpu.VMEM((2, 2, NY * rows, width), bf16),
            pltpu.VMEM((2, 2, (NY - 1) * rows, width), bf16),
            pltpu.VMEM((2, 2, NY * rows, width), bf16),
            pltpu.VMEM((NZ, 8, tok), jnp.float32),
            pltpu.VMEM((2, tok, width), bf16),
            pltpu.VMEM((2, tok, width), bf16),
            pltpu.VMEM((width, hidden), bf16),
            pltpu.VMEM((hidden, width), bf16),
            pltpu.VMEM((2, NY * rows, hidden), bf16),
            pltpu.VMEM((2, NY * rows, hidden), jnp.float32),
            pltpu.VMEM((2, NZ, tok, NY * rows), bf16),
            dma((2, 2, 4, 4)), dma((2, 2, 4, 4)),
            dma((2, 4)), dma((2, 4)),
            dma((2, 2, 2, 3)), dma((2, 2, 2, 3)),
            dma((2, 2, 2, 3)), dma((2, 2, 2, 3)),
            dma((2, 2, 4, 4)), dma((2, 2, 4, 4)),
            dma((2, 4)), dma((2, 4)),
            dma((4,)),
            pltpu.SemaphoreType.REGULAR((2,)),
        ],
        compiler_params=pltpu.CompilerParams(
            collective_id=0, has_side_effects=True, vmem_limit_bytes=62 * 1024 * 1024
        ),
        cost_estimate=pl.CostEstimate(
            flops=2 * 2 * 2 * NZ * NY * cap * width * hidden,
            bytes_accessed=16 * 1024 * 1024,
            transcendentals=0,
        ),
    )(xf, xr, norm_gain, upper, lower, info)
    return outf[None], outr[None]


def solution(mesh):
    return jax.shard_map(
        shards,
        mesh=mesh,
        in_specs=(
            P("pipe", "expert", None),
            P("pipe", "expert", None),
            P("pipe", None),
            P("pipe", "expert", None, None),
            P("pipe", "expert", None, None),
            P("pipe", None, "expert", None),
            P("pipe", None, "expert", None),
        ),
        out_specs=(P("pipe", "expert", None), P("pipe", "expert", None)),
        check_vma=False,
    )
```

```python
import functools

import jax
import jax.numpy as jnp
from jax import lax
from jax.experimental import pallas as pl
from jax.experimental.pallas import tpu as pltpu
from jax.sharding import PartitionSpec as P

SPLIT = 2
TOPK = 2
NY = 4
NZ = 8
GROUP = 4
MESH = pl.DeviceIdType.MESH

IN, OUT = 0, 1
NEAR, FAR = 0, 1


def tile_of(width, most=512):
    tile = 128
    for t in range(128, most + 1, 128):
        if width % t == 0:
            tile = t
    return tile


def kernel(
    cap,
    xf_hbm, xr_hbm, gain_ref, up_hbm, down_hbm, info_ref,
    outf_ref, outr_ref,
    ag, pkd, stag, tmp, inc, sel, ret, infos, xs, stage, up, down, act, hid,
    gmat, order, leaf, pack, spread,
    ag_send, ag_recv, inf_send, inf_recv, yd_send, yd_recv, yr_send, yr_recv,
    rs_send, rs_recv, sh_send, sh_recv, load_sem, credit,
):
    tok, width = xs.shape[1], xs.shape[2]
    half = width // 2
    quarter = width // 4
    rows = GROUP * cap
    slots = NY * cap
    per_y = NZ // SPLIT
    experts = NY * per_y
    p = lax.axis_index("pipe")
    e = lax.axis_index("expert")
    n_pipe = lax.axis_size("pipe")
    y, z = e // NZ, e % NZ
    odd = z % 2
    z_in = z + 1 - 2 * odd
    z_out = (z + NZ - 1 + 2 * odd) % NZ
    zdev = {IN: (p, y * NZ + z_in), OUT: (p, y * NZ + z_out)}
    ydev = {d: (p, ((y + d) % NY) * NZ + z) for d in (1, 2, 3)}
    pdev = {0: ((p + 1) % n_pipe, e), 1: ((p + n_pipe - 1) % n_pipe, e)}
    outs = {0: outf_ref, 1: outr_ref}

    def remote(src, dst, send, recv, device):
        return pltpu.make_async_remote_copy(
            src_ref=src, dst_ref=dst, send_sem=send, recv_sem=recv,
            device_id=device, device_id_type=MESH,
        )

    def chunk(c):
        return pl.ds(c * quarter, quarter)

    barrier = pltpu.get_barrier_semaphore()
    peers = [zdev[0], zdev[1], ydev[1], ydev[2], ydev[3], pdev[0], pdev[1]]
    for device in peers:
        pl.semaphore_signal(barrier, inc=1, device_id=device, device_id_type=MESH)

    load_xf = pltpu.make_async_copy(xf_hbm, xs.at[0], load_sem.at[0])
    load_xr = pltpu.make_async_copy(xr_hbm, xs.at[1], load_sem.at[1])
    load_up = pltpu.make_async_copy(up_hbm, up, load_sem.at[2])
    load_down = pltpu.make_async_copy(down_hbm, down, load_sem.at[3])

    def normalise(s):
        gain = gain_ref[...].astype(jnp.float32)

        def body(i, carry):
            at = pl.ds(pl.multiple_of(i * 16, 16), 16)
            x = xs[s, at, :].astype(jnp.float32)
            scale = lax.rsqrt(jnp.mean(x * x, axis=-1, keepdims=True) + 1e-06)
            ag[s, 0, at, :] = (x * scale * gain).astype(jnp.bfloat16)
            return carry

        lax.fori_loop(0, tok // 16, body, 0)

    def own_info():
        here = lax.broadcasted_iota(jnp.int32, (experts, tok), 0).astype(jnp.float32)
        t0 = lax.broadcasted_iota(jnp.int32, (tok, tok), 0)
        t1 = lax.broadcasted_iota(jnp.int32, (tok, tok), 1)
        earlier = jnp.where(t0 < t1, 1.0, 0.0).astype(jnp.bfloat16)
        for s in (0, 1):
            hits = [here == info_ref[4 * s + k : 4 * s + k + 1, :] for k in range(TOPK)]
            named = jnp.where(hits[0] | hits[1], 1.0, 0.0).astype(jnp.bfloat16)
            before = jnp.dot(named, earlier, preferred_element_type=jnp.float32)
            for k in range(TOPK):
                code = jnp.where(hits[k], here * cap + before, 0.0)
                infos[0, 4 * s + k : 4 * s + k + 1, :] = jnp.sum(code, axis=0, keepdims=True)
            infos[0, 4 * s + 2 : 4 * s + 4, :] = info_ref[4 * s + 2 : 4 * s + 4, :]

    def ag_copy(s, way, hop, c):
        if way == IN:
            buf, src, dst = {
                1: (ag, ag.at[s, 0], 2), 2: (ag, ag.at[s, 1], 3),
                3: (pkd, pkd.at[s, 0], 2), 4: (pkd, pkd.at[s, 1], 3),
            }[hop]
        else:
            buf, src, dst = {
                1: (ag, ag.at[s, 0], 1), 2: (pkd, stag.at[s, 0], 0), 3: (pkd, stag.at[s, 1], 1),
            }[hop]
        return remote(
            src.at[:, chunk(c)], buf.at[s, dst, :, chunk(c)],
            ag_send.at[s, way, hop - 1, c], ag_recv.at[s, way, hop - 1, c], zdev[way],
        )

    INFO = ((IN, 0, 2), (OUT, 0, 1), (IN, 1, 3))

    def inf_copy(i):
        way, source, target = INFO[i]
        return remote(infos.at[source], infos.at[target], inf_send.at[i], inf_recv.at[i], zdev[way])

    def chunks(h):
        return (2 * h, 2 * h + 1)

    def own_send(s, h, ways):
        for c in chunks(h):
            for way in ways:
                ag_copy(s, way, 1, c).start()

    def pack_send(s, far, c):
        block = jnp.dot(pack[s, far], ag[s, 2 + far, :, chunk(c)], preferred_element_type=jnp.float32)
        stag[s, far, :, chunk(c)] = block.astype(jnp.bfloat16)
        ag_copy(s, OUT, 2 + far, c).start()

    def second_hop(s, h):
        for c in chunks(h):
            ag_copy(s, OUT, 1, c).wait_recv()
            ag_copy(s, IN, 2, c).start()
            ag_copy(s, IN, 1, c).wait_recv()
            pack_send(s, 0, c)

    def third_hop(s, h):
        for c in chunks(h):
            ag_copy(s, OUT, 2, c).wait_recv()
            ag_copy(s, IN, 3, c).start()
            ag_copy(s, IN, 2, c).wait_recv()
            pack_send(s, 1, c)

    def fourth_hop(s, h):
        for c in chunks(h):
            ag_copy(s, OUT, 3, c).wait_recv()
            ag_copy(s, IN, 4, c).start()

    def gather_end(s, h):
        for hop in (3, 4):
            for c in chunks(h):
                ag_copy(s, IN, hop, c).wait_recv()

    def gather_sent(s):
        for c in range(4):
            for hop in (1, 2, 3, 4):
                ag_copy(s, IN, hop, c).wait_send()
            for hop in (1, 2, 3):
                ag_copy(s, OUT, hop, c).wait_send()

    def split_rows(shape):
        r = lax.broadcasted_iota(jnp.int32, shape, 0)
        one, zero = jnp.int32(1), jnp.int32(0)
        u = sum(jnp.where(r >= k * rows, one, zero) for k in (1, 2, 3))
        r = r - u * rows
        v = sum(jnp.where(r >= k * cap, one, zero) for k in (1, 2, 3))
        return u, v, r - v * cap

    def expert_at(d, pair):
        yd = y + d
        yd = yd - jnp.where(yd >= NY, jnp.int32(NY), jnp.int32(0))
        return yd * per_y + pair

    def constants():
        d, i, c = split_rows((NY * rows, NY * rows))
        column = lax.broadcasted_iota(jnp.int32, (NY * rows, NY * rows), 1)
        order[...] = jnp.where(column == i * slots + d * cap + c, 1.0, 0.0).astype(jnp.bfloat16)
        _, d, c = split_rows((slots, NY * rows))
        column = lax.broadcasted_iota(jnp.int32, (slots, NY * rows), 1)
        for i in range(GROUP):
            leaf[i] = jnp.where(column == d * rows + i * cap + c, 1.0, 0.0).astype(jnp.bfloat16)

    def hits_of(s, info, codes):
        hit0 = codes == info[4 * s : 4 * s + 1, :]
        hit1 = codes == info[4 * s + 1 : 4 * s + 2, :]
        weights = jnp.where(hit0, info[4 * s + 2 : 4 * s + 3, :], 0.0) + jnp.where(
            hit1, info[4 * s + 3 : 4 * s + 4, :], 0.0
        )
        return jnp.where(hit0 | hit1, 1.0, 0.0).astype(jnp.bfloat16), weights.T.astype(jnp.bfloat16)

    def pack_matrices(far):
        _, d, c = split_rows((slots, tok))
        codes = (expert_at(d, z_out // SPLIT) * cap + c).astype(jnp.float32)
        info = infos[2 + far]
        for s in (0, 1):
            pack[s, far], spread[s, far] = hits_of(s, info, codes)

    def select(s, h, g):
        if g == NEAR:
            d, at, c = split_rows((NY * rows, tok))
            codes = (expert_at(d, z // SPLIT) * cap + c).astype(jnp.float32)
            parts = []
            for i in range(GROUP):
                mine, weights = hits_of(s, infos[i], jnp.where(at == i, codes, -1.0))
                parts.append(mine)
                if h == 0:
                    gmat[s, i] = weights
            pick = jnp.concatenate(parts, axis=1)
            source, depth = ag, tok
        else:
            pick = order[...]
            source, depth = pkd, slots
        tile = tile_of(half)

        def body(j, carry):
            cols = pl.ds(pl.multiple_of(h * half + j * tile, 128), tile)
            block = source[s, :, :, cols].reshape(GROUP * depth, tile)
            out = jnp.dot(pick, block, preferred_element_type=jnp.float32).astype(jnp.bfloat16)
            inc[s, g, 0:rows, cols] = out[0:rows]
            sel[s, g, :, cols] = out[rows:]
            return carry

        lax.fori_loop(0, half // tile, body, 0)
        for d in (1, 2, 3):
            yd_copy(s, h, g, d).start()

    def yd_copy(s, h, g, d):
        cols = pl.ds(h * half, half)
        return remote(
            sel.at[s, g, pl.ds((d - 1) * rows, rows), cols],
            inc.at[s, g, pl.ds(d * rows, rows), cols],
            yd_send.at[s, h, g, d - 1], yd_recv.at[s, h, g, d - 1], ydev[d],
        )

    def yr_copy(s, h, g, d):
        cols = pl.ds(h * half, half)
        block = pl.ds(d * rows, rows)
        return remote(
            inc.at[s, g, block, cols], ret.at[s, g, block, cols],
            yr_send.at[s, h, g, d - 1], yr_recv.at[s, h, g, d - 1], ydev[NY - d],
        )

    def back(s, h, g):
        for d in (1, 2, 3):
            yr_copy(s, h, g, d).wait_recv()

    def upper(s, h, g):
        for d in (1, 2, 3):
            yd_copy(s, h, g, d).wait_recv()
        tile = tile_of(half)
        if h == 0:
            hid[g] = jnp.zeros(hid.shape[1:], jnp.float32)

        def body(j, carry):
            cols = pl.ds(pl.multiple_of(h * half + j * tile, 128), tile)
            hid[g] += jnp.dot(inc[s, g, :, cols], up[cols, :], preferred_element_type=jnp.float32)
            return carry

        lax.fori_loop(0, half // tile, body, 0)
        if h == 1:
            act[g] = jax.nn.silu(hid[g]).astype(jnp.bfloat16)

    def lower(s, h, g):
        tile = tile_of(half)

        def body(j, carry):
            cols = pl.ds(pl.multiple_of(h * half + j * tile, 128), tile)
            out = jnp.dot(act[g], down[:, cols], preferred_element_type=jnp.float32)
            out = out.astype(jnp.bfloat16)
            ret[s, g, 0:rows, cols] = out[0:rows]
            inc[s, g, rows:, cols] = out[rows:]
            return carry

        lax.fori_loop(0, half // tile, body, 0)
        for d in (2, 1, 3):
            yr_copy(s, h, g, d).start()

    def rs_copy(s, way, step, c):
        if way == IN:
            buf, src, dst = {
                0: (pkd, stag.at[s, 0], 1), 1: (pkd, stag.at[s, 1], 0),
                2: (ag, ag.at[s, 3], 1), 3: (ag, tmp.at[s], 0),
            }[step]
        else:
            buf, src, dst = {
                0: (pkd, pkd.at[s, 1], 2), 1: (pkd, pkd.at[s, 0], 3), 2: (ag, ag.at[s, 1], 2),
            }[step]
        return remote(
            src.at[:, chunk(c)], buf.at[s, dst, :, chunk(c)],
            rs_send.at[s, way, step, c], rs_recv.at[s, way, step, c], zdev[way],
        )

    def near_rows(s, i, c):
        return jnp.dot(gmat[s, i], ret[s, NEAR, :, chunk(c)], preferred_element_type=jnp.float32)

    def far_rows(s, i, c):
        return jnp.dot(leaf[i], ret[s, FAR, :, chunk(c)], preferred_element_type=jnp.float32)

    def rs_begin(s, h):
        for step, i in ((0, 3), (1, 2)):
            for c in chunks(h):
                stag[s, step, :, chunk(c)] = far_rows(s, i, c).astype(jnp.bfloat16)
                rs_copy(s, IN, step, c).start()

    def pair_sum(s, step, c):
        own = far_rows(s, 1 - step, c)
        rs_copy(s, IN, step, c).wait_recv()
        total = own + pkd[s, 1 - step, :, chunk(c)].astype(jnp.float32)
        pkd[s, 1 - step, :, chunk(c)] = total.astype(jnp.bfloat16)
        rs_copy(s, OUT, step, c).start()

    def spread_sum(s, step, c):
        own = near_rows(s, 3 - step, c)
        rs_copy(s, OUT, step, c).wait_recv()
        total = own + jnp.dot(
            spread[s, 1 - step], pkd[s, 2 + step, :, chunk(c)], preferred_element_type=jnp.float32
        )
        if step == 0:
            ag[s, 3, :, chunk(c)] = total.astype(jnp.bfloat16)
        else:
            tmp[s, :, chunk(c)] = total.astype(jnp.bfloat16)
        rs_copy(s, IN, 2 + step, c).start()

    def pass_sum(s, c):
        own = near_rows(s, 1, c)
        rs_copy(s, IN, 2, c).wait_recv()
        total = own + ag[s, 1, :, chunk(c)].astype(jnp.float32)
        ag[s, 1, :, chunk(c)] = total.astype(jnp.bfloat16)
        rs_copy(s, OUT, 2, c).start()

    def rs_mid_a(s, h):
        for c in chunks(h):
            pair_sum(s, 0, c)

    def rs_mid_b(s, h):
        for c in chunks(h):
            spread_sum(s, 0, c)
            pair_sum(s, 1, c)

    def rs_late_a(s, h):
        for c in chunks(h):
            spread_sum(s, 1, c)

    def rs_late_b(s, h):
        for c in chunks(h):
            pass_sum(s, c)

    def sh_copy(s, c):
        return remote(
            stage.at[s, :, chunk(c)], outs[s].at[:, chunk(c)], sh_send.at[s, c], sh_recv.at[s, c], pdev[s]
        )

    def rs_end(s, h):
        for c in chunks(h):
            own = near_rows(s, 0, c) + xs[s, :, chunk(c)].astype(jnp.float32)
            rs_copy(s, OUT, 2, c).wait_recv()
            rs_copy(s, IN, 3, c).wait_recv()
            total = own + (
                ag[s, 0, :, chunk(c)].astype(jnp.float32) + ag[s, 2, :, chunk(c)].astype(jnp.float32)
            )
            stage[s, :, chunk(c)] = total.astype(jnp.bfloat16)
            sh_copy(s, c).start()

    def finish(s):
        for h in (0, 1):
            for g in (0, 1):
                for d in (1, 2, 3):
                    yd_copy(s, h, g, d).wait_send()
                    yr_copy(s, h, g, d).wait_send()
        for c in range(4):
            for step in (0, 1, 2, 3):
                rs_copy(s, IN, step, c).wait_send()
            for step in (0, 1, 2):
                rs_copy(s, OUT, step, c).wait_send()
            sh_copy(s, c).wait()

    def give_credit(s):
        gather_sent(s)
        for way in (IN, OUT):
            pl.semaphore_signal(credit.at[s], inc=1, device_id=zdev[way], device_id_type=MESH)

    f, r, near, far = 0, 1, NEAR, FAR
    both = (IN, OUT)

    load_xf.start()
    load_xr.start()
    own_info()
    load_xf.wait()
    normalise(f)
    pl.semaphore_wait(barrier, len(peers))

    inf_copy(0).start()
    inf_copy(1).start()
    own_send(f, 0, (IN,))
    own_send(f, 0, (OUT,))
    constants()
    load_up.start()
    load_down.start()
    inf_copy(1).wait_recv()
    inf_copy(2).start()
    inf_copy(0).wait_recv()
    pack_matrices(0)
    second_hop(f, 0)
    inf_copy(2).wait_recv()
    pack_matrices(1)
    third_hop(f, 0)
    select(f, 0, near)
    fourth_hop(f, 0)
    own_send(f, 1, (OUT,))
    own_send(f, 1, (IN,))
    load_xr.wait()
    normalise(r)
    gather_end(f, 0)
    select(f, 0, far)
    second_hop(f, 1)
    third_hop(f, 1)
    select(f, 1, near)
    fourth_hop(f, 1)
    load_up.wait()
    load_down.wait()
    upper(f, 0, near)
    own_send(r, 0, (OUT,))
    own_send(r, 1, (OUT,))
    own_send(r, 0, (IN,))
    gather_end(f, 1)
    select(f, 1, far)
    own_send(r, 1, (IN,))
    upper(f, 0, far)
    upper(f, 1, near)
    lower(f, 1, near)
    upper(f, 1, far)
    lower(f, 1, far)
    second_hop(r, 1)
    lower(f, 0, far)
    second_hop(r, 0)
    third_hop(r, 0)
    fourth_hop(r, 0)
    third_hop(r, 1)
    select(r, 0, near)
    fourth_hop(r, 1)
    gather_end(r, 0)
    give_credit(f)
    lower(f, 0, near)
    back(f, 1, far)
    select(r, 0, far)
    back(f, 0, far)
    back(f, 1, near)
    pl.semaphore_wait(credit.at[f], 2)
    rs_begin(f, 0)
    gather_end(r, 1)
    rs_mid_a(f, 0)
    upper(r, 0, near)
    rs_begin(f, 1)
    select(r, 1, far)
    back(f, 0, near)
    rs_mid_a(f, 1)
    rs_mid_b(f, 0)
    rs_mid_b(f, 1)
    select(r, 1, near)
    upper(r, 0, far)
    rs_late_a(f, 1)
    upper(r, 1, far)
    lower(r, 0, far)
    rs_late_b(f, 1)
    upper(r, 1, near)
    give_credit(r)
    rs_late_a(f, 0)
    lower(r, 0, near)
    rs_end(f, 1)
    rs_late_b(f, 0)
    back(r, 0, far)
    pl.semaphore_wait(credit.at[r], 2)
    rs_begin(r, 0)
    rs_mid_a(r, 0)
    lower(r, 1, far)
    back(r, 0, near)
    rs_mid_b(r, 0)
    rs_late_a(r, 0)
    rs_late_b(r, 0)
    lower(r, 1, near)
    back(r, 1, far)
    rs_begin(r, 1)
    rs_mid_a(r, 1)
    rs_end(f, 0)
    back(r, 1, near)
    rs_mid_b(r, 1)
    rs_late_a(r, 1)
    rs_late_b(r, 1)
    rs_end(r, 0)
    rs_end(r, 1)
    for i in range(len(INFO)):
        inf_copy(i).wait_send()
    finish(f)
    finish(r)


def shards(stream_fwd, stream_rev, norm_gain, w_up, w_down, routes, gates):
    xf, xr = stream_fwd[0], stream_rev[0]
    upper, lower = w_up[0, 0], w_down[0, 0]
    tok, width = xf.shape
    hidden = upper.shape[1]
    experts = lax.axis_size("expert") // SPLIT
    cap = SPLIT * max(1, tok * TOPK * 5 // (4 * SPLIT * experts))
    info = jnp.concatenate([routes[0].astype(jnp.float32), gates[0].astype(jnp.float32)], axis=-1)
    info = info.transpose(0, 2, 1).reshape(8, tok)
    rows = GROUP * cap
    bf16 = jnp.bfloat16
    dma = pltpu.SemaphoreType.DMA
    anywhere = pl.BlockSpec(memory_space=pl.ANY)
    in_vmem = pl.BlockSpec(memory_space=pltpu.VMEM)
    outf, outr = pl.pallas_call(
        functools.partial(kernel, cap),
        out_shape=(jax.ShapeDtypeStruct((tok, width), bf16),) * 2,
        in_specs=[anywhere, anywhere, in_vmem, anywhere, anywhere, in_vmem],
        out_specs=(anywhere, anywhere),
        scratch_shapes=[
            pltpu.VMEM((2, GROUP, tok, width), bf16),
            pltpu.VMEM((2, GROUP, NY * cap, width), bf16),
            pltpu.VMEM((2, 2, NY * cap, width), bf16),
            pltpu.VMEM((2, tok, width), bf16),
            pltpu.VMEM((2, 2, NY * rows, width), bf16),
            pltpu.VMEM((2, 2, (NY - 1) * rows, width), bf16),
            pltpu.VMEM((2, 2, NY * rows, width), bf16),
            pltpu.VMEM((GROUP, 8, tok), jnp.float32),
            pltpu.VMEM((2, tok, width), bf16),
            pltpu.VMEM((2, tok, width), bf16),
            pltpu.VMEM((width, hidden), bf16),
            pltpu.VMEM((hidden, width), bf16),
            pltpu.VMEM((2, NY * rows, hidden), bf16),
            pltpu.VMEM((2, NY * rows, hidden), jnp.float32),
            pltpu.VMEM((2, GROUP, tok, NY * rows), bf16),
            pltpu.VMEM((NY * rows, NY * rows), bf16),
            pltpu.VMEM((GROUP, NY * cap, NY * rows), bf16),
            pltpu.VMEM((2, 2, NY * cap, tok), bf16),
            pltpu.VMEM((2, 2, tok, NY * cap), bf16),
            dma((2, 2, 4, 4)), dma((2, 2, 4, 4)),
            dma((3,)), dma((3,)),
            dma((2, 2, 2, 3)), dma((2, 2, 2, 3)),
            dma((2, 2, 2, 3)), dma((2, 2, 2, 3)),
            dma((2, 2, 4, 4)), dma((2, 2, 4, 4)),
            dma((2, 4)), dma((2, 4)),
            dma((4,)),
            pltpu.SemaphoreType.REGULAR((2,)),
        ],
        compiler_params=pltpu.CompilerParams(
            collective_id=0, has_side_effects=True, vmem_limit_bytes=62 * 1024 * 1024
        ),
        cost_estimate=pl.CostEstimate(
            flops=2 * 2 * 2 * NZ * NY * cap * width * hidden,
            bytes_accessed=16 * 1024 * 1024,
            transcendentals=0,
        ),
    )(xf, xr, norm_gain, upper, lower, info)
    return outf[None], outr[None]


def solution(mesh):
    return jax.shard_map(
        shards,
        mesh=mesh,
        in_specs=(
            P("pipe", "expert", None),
            P("pipe", "expert", None),
            P("pipe", None),
            P("pipe", "expert", None, None),
            P("pipe", "expert", None, None),
            P("pipe", None, "expert", None),
            P("pipe", None, "expert", None),
        ),
        out_specs=(P("pipe", "expert", None), P("pipe", "expert", None)),
        check_vma=False,
    )
```

```python
import functools

import jax
import jax.numpy as jnp
from jax import lax
from jax.experimental import pallas as pl
from jax.experimental.pallas import tpu as pltpu
from jax.sharding import PartitionSpec as P

SPLIT = 2
TOPK = 2
NY = 4
NZ = 8
GROUP = 4
MESH = pl.DeviceIdType.MESH

IN, OUT = 0, 1
NEAR, FAR = 0, 1


def tile_of(width, most=512):
    tile = 128
    for t in range(128, most + 1, 128):
        if width % t == 0:
            tile = t
    return tile


def kernel(
    cap,
    xf_hbm, xr_hbm, gain_ref, up_hbm, down_hbm, info_ref,
    outf_ref, outr_ref,
    ag, pkd, stag, swap, tmp, inc, sel, ret, infos, xs, stage, up, down, act, parted, hid,
    gmat, order, part, widen, leaf, pack, spread,
    ag_send, ag_recv, inf_send, inf_recv, yd_send, yd_recv, yr_send, yr_recv,
    rs_send, rs_recv, sh_send, sh_recv, load_sem, credit,
):
    tok, width = xs.shape[1], xs.shape[2]
    half = width // 2
    quarter = width // 4
    rows = GROUP * cap
    slots = NY * cap
    kept = parted.shape[0] - 2 * slots
    pad = kept // NY
    per_y = NZ // SPLIT
    experts = NY * per_y
    p = lax.axis_index("pipe")
    e = lax.axis_index("expert")
    n_pipe = lax.axis_size("pipe")
    y, z = e // NZ, e % NZ
    odd = z % 2
    z_in = z + 1 - 2 * odd
    z_out = (z + NZ - 1 + 2 * odd) % NZ
    zdev = {IN: (p, y * NZ + z_in), OUT: (p, y * NZ + z_out)}
    ydev = {d: (p, ((y + d) % NY) * NZ + z) for d in (1, 2, 3)}
    pdev = {0: ((p + 1) % n_pipe, e), 1: ((p + n_pipe - 1) % n_pipe, e)}
    outs = {0: outf_ref, 1: outr_ref}

    def remote(src, dst, send, recv, device):
        return pltpu.make_async_remote_copy(
            src_ref=src, dst_ref=dst, send_sem=send, recv_sem=recv,
            device_id=device, device_id_type=MESH,
        )

    def chunk(c):
        return pl.ds(c * quarter, quarter)

    barrier = pltpu.get_barrier_semaphore()
    peers = [zdev[0], zdev[1], ydev[1], ydev[2], ydev[3], pdev[0], pdev[1]]
    for device in peers:
        pl.semaphore_signal(barrier, inc=1, device_id=device, device_id_type=MESH)

    load_xf = pltpu.make_async_copy(xf_hbm, xs.at[0], load_sem.at[0])
    load_xr = pltpu.make_async_copy(xr_hbm, xs.at[1], load_sem.at[1])
    load_up = pltpu.make_async_copy(up_hbm, up, load_sem.at[2])
    load_down = pltpu.make_async_copy(down_hbm, down, load_sem.at[3])

    def normalise(s):
        gain = gain_ref[...].astype(jnp.float32)

        def body(i, carry):
            at = pl.ds(pl.multiple_of(i * 16, 16), 16)
            x = xs[s, at, :].astype(jnp.float32)
            scale = lax.rsqrt(jnp.mean(x * x, axis=-1, keepdims=True) + 1e-06)
            ag[s, 0, at, :] = (x * scale * gain).astype(jnp.bfloat16)
            return carry

        lax.fori_loop(0, tok // 16, body, 0)

    def own_info():
        here = lax.broadcasted_iota(jnp.int32, (experts, tok), 0).astype(jnp.float32)
        t0 = lax.broadcasted_iota(jnp.int32, (tok, tok), 0)
        t1 = lax.broadcasted_iota(jnp.int32, (tok, tok), 1)
        earlier = jnp.where(t0 < t1, 1.0, 0.0).astype(jnp.bfloat16)
        for s in (0, 1):
            hits = [here == info_ref[4 * s + k : 4 * s + k + 1, :] for k in range(TOPK)]
            named = jnp.where(hits[0] | hits[1], 1.0, 0.0).astype(jnp.bfloat16)
            before = jnp.dot(named, earlier, preferred_element_type=jnp.float32)
            for k in range(TOPK):
                code = jnp.where(hits[k], here * cap + before, 0.0)
                infos[0, 4 * s + k : 4 * s + k + 1, :] = jnp.sum(code, axis=0, keepdims=True)
            infos[0, 4 * s + 2 : 4 * s + 4, :] = info_ref[4 * s + 2 : 4 * s + 4, :]

    def ag_copy(s, way, hop, c):
        if way == IN:
            buf, src, dst = {
                1: (ag, ag.at[s, 0], 2), 2: (ag, ag.at[s, 1], 3),
                3: (pkd, pkd.at[s, 0], 2), 4: (pkd, pkd.at[s, 1], 3),
            }[hop]
        else:
            buf, src, dst = {
                1: (ag, ag.at[s, 0], 1),
                2: (pkd, stag.at[s, 0:slots], 0),
                3: (pkd, stag.at[s, slots : 2 * slots], 1),
            }[hop]
        return remote(
            src.at[:, chunk(c)], buf.at[s, dst, :, chunk(c)],
            ag_send.at[s, way, hop - 1, c], ag_recv.at[s, way, hop - 1, c], zdev[way],
        )

    INFO = ((IN, 0, 2), (OUT, 0, 1), (IN, 1, 3))

    def inf_copy(i):
        way, source, target = INFO[i]
        return remote(infos.at[source], infos.at[target], inf_send.at[i], inf_recv.at[i], zdev[way])

    def chunks(h):
        return (2 * h, 2 * h + 1)

    def own_send(s, h, ways):
        for c in chunks(h):
            for way in ways:
                ag_copy(s, way, 1, c).start()

    def pack_send(s, far, c):
        block = jnp.dot(pack[s, far], ag[s, 2 + far, :, chunk(c)], preferred_element_type=jnp.float32)
        stag[s, far * slots : (far + 1) * slots, chunk(c)] = block.astype(jnp.bfloat16)
        ag_copy(s, OUT, 2 + far, c).start()

    def second_hop(s, h):
        for c in chunks(h):
            ag_copy(s, OUT, 1, c).wait_recv()
            ag_copy(s, IN, 2, c).start()
            ag_copy(s, IN, 1, c).wait_recv()
            pack_send(s, 0, c)

    def third_hop(s, h):
        for c in chunks(h):
            ag_copy(s, OUT, 2, c).wait_recv()
            ag_copy(s, IN, 3, c).start()
            ag_copy(s, IN, 2, c).wait_recv()
            pack_send(s, 1, c)

    def fourth_hop(s, h):
        for c in chunks(h):
            ag_copy(s, OUT, 3, c).wait_recv()
            ag_copy(s, IN, 4, c).start()

    def gather_end(s, h):
        for hop in (3, 4):
            for c in chunks(h):
                ag_copy(s, IN, hop, c).wait_recv()

    def gather_sent(s):
        for c in range(4):
            for hop in (1, 2, 3, 4):
                ag_copy(s, IN, hop, c).wait_send()
            for hop in (1, 2, 3):
                ag_copy(s, OUT, hop, c).wait_send()

    def split_rows(shape):
        r = lax.broadcasted_iota(jnp.int32, shape, 0)
        one, zero = jnp.int32(1), jnp.int32(0)
        u = sum(jnp.where(r >= k * rows, one, zero) for k in (1, 2, 3))
        r = r - u * rows
        v = sum(jnp.where(r >= k * cap, one, zero) for k in (1, 2, 3))
        return u, v, r - v * cap

    def expert_at(d, pair):
        yd = y + d
        yd = yd - jnp.where(yd >= NY, jnp.int32(NY), jnp.int32(0))
        return yd * per_y + pair

    def constants():
        d, i, c = split_rows((NY * rows, NY * rows))
        column = lax.broadcasted_iota(jnp.int32, (NY * rows, NY * rows), 1)
        order[...] = jnp.where(column == i * slots + d * cap + c, 1.0, 0.0).astype(jnp.bfloat16)
        r = lax.broadcasted_iota(jnp.int32, (kept, NY * rows), 0)
        column = lax.broadcasted_iota(jnp.int32, (kept, NY * rows), 1)
        d = sum(jnp.where(r >= k * pad, jnp.int32(1), jnp.int32(0)) for k in (1, 2, 3))
        q = r - d * pad
        part[0:kept] = jnp.where((column == d * rows + q) & (q < 2 * cap), 1.0, 0.0).astype(jnp.bfloat16)
        r = lax.broadcasted_iota(jnp.int32, (2 * slots, NY * rows), 0)
        column = lax.broadcasted_iota(jnp.int32, (2 * slots, NY * rows), 1)
        d = sum(jnp.where(r >= k * 2 * cap, jnp.int32(1), jnp.int32(0)) for k in (1, 2, 3))
        q = r - d * 2 * cap
        part[kept:] = jnp.where(column == d * rows + 2 * cap + q, 1.0, 0.0).astype(jnp.bfloat16)
        r = lax.broadcasted_iota(jnp.int32, (kept, 2 * slots), 0)
        column = lax.broadcasted_iota(jnp.int32, (kept, 2 * slots), 1)
        d = sum(jnp.where(r >= k * pad, jnp.int32(1), jnp.int32(0)) for k in (1, 2, 3))
        q = r - d * pad
        widen[...] = jnp.where((column == d * 2 * cap + q) & (q < 2 * cap), 1.0, 0.0).astype(jnp.bfloat16)
        _, d, c = split_rows((slots, kept))
        column = lax.broadcasted_iota(jnp.int32, (slots, kept), 1)
        for i in (0, 1):
            leaf[i] = jnp.where(column == d * pad + i * cap + c, 1.0, 0.0).astype(jnp.bfloat16)

    def hits_of(s, info, codes):
        hit0 = codes == info[4 * s : 4 * s + 1, :]
        hit1 = codes == info[4 * s + 1 : 4 * s + 2, :]
        weights = jnp.where(hit0, info[4 * s + 2 : 4 * s + 3, :], 0.0) + jnp.where(
            hit1, info[4 * s + 3 : 4 * s + 4, :], 0.0
        )
        return jnp.where(hit0 | hit1, 1.0, 0.0).astype(jnp.bfloat16), weights.T.astype(jnp.bfloat16)

    def pack_matrices(far):
        _, d, c = split_rows((slots, tok))
        codes = (expert_at(d, z_out // SPLIT) * cap + c).astype(jnp.float32)
        info = infos[2 + far]
        for s in (0, 1):
            pack[s, far], spread[s, far] = hits_of(s, info, codes)

    def select(s, h, g):
        if g == NEAR:
            d, at, c = split_rows((NY * rows, tok))
            codes = (expert_at(d, z // SPLIT) * cap + c).astype(jnp.float32)
            parts = []
            for i in range(GROUP):
                mine, weights = hits_of(s, infos[i], jnp.where(at == i, codes, -1.0))
                parts.append(mine)
                if h == 0:
                    gmat[s, i] = weights
            pick = jnp.concatenate(parts, axis=1)
            source, depth = ag, tok
        else:
            pick = order[...]
            source, depth = pkd, slots
        tile = tile_of(half)

        def body(j, carry):
            cols = pl.ds(pl.multiple_of(h * half + j * tile, 128), tile)
            block = source[s, :, :, cols].reshape(GROUP * depth, tile)
            out = jnp.dot(pick, block, preferred_element_type=jnp.float32).astype(jnp.bfloat16)
            inc[s, g, 0:rows, cols] = out[0:rows]
            sel[s, g, :, cols] = out[rows:]
            return carry

        lax.fori_loop(0, half // tile, body, 0)
        for d in (1, 2, 3):
            yd_copy(s, h, g, d).start()

    def yd_copy(s, h, g, d):
        cols = pl.ds(h * half, half)
        return remote(
            sel.at[s, g, pl.ds((d - 1) * rows, rows), cols],
            inc.at[s, g, pl.ds(d * rows, rows), cols],
            yd_send.at[s, h, g, d - 1], yd_recv.at[s, h, g, d - 1], ydev[d],
        )

    def yr_copy(s, h, g, d):
        cols = pl.ds(h * half, half)
        many = rows if g == NEAR else pad
        block = pl.ds(d * many, many)
        return remote(
            inc.at[s, g, block, cols], ret.at[s, g, block, cols],
            yr_send.at[s, h, g, d - 1], yr_recv.at[s, h, g, d - 1], ydev[NY - d],
        )

    def back(s, h, g):
        for d in (1, 2, 3):
            yr_copy(s, h, g, d).wait_recv()

    def upper(s, h, g):
        for d in (1, 2, 3):
            yd_copy(s, h, g, d).wait_recv()
        tile = tile_of(half)
        if h == 0:
            hid[g] = jnp.zeros(hid.shape[1:], jnp.float32)

        def body(j, carry):
            cols = pl.ds(pl.multiple_of(h * half + j * tile, 128), tile)
            hid[g] += jnp.dot(inc[s, g, :, cols], up[cols, :], preferred_element_type=jnp.float32)
            return carry

        lax.fori_loop(0, half // tile, body, 0)
        if h == 1:
            value = jax.nn.silu(hid[g]).astype(jnp.bfloat16)
            if g == NEAR:
                act[...] = value
            else:
                parted[...] = jnp.dot(part[...], value, preferred_element_type=jnp.float32).astype(
                    jnp.bfloat16
                )

    def lower(s, h, g):
        tile = tile_of(half)

        def body(j, carry):
            cols = pl.ds(pl.multiple_of(h * half + j * tile, 128), tile)
            source = act if g == NEAR else parted
            out = jnp.dot(source[...], down[:, cols], preferred_element_type=jnp.float32)
            out = out.astype(jnp.bfloat16)
            if g == NEAR:
                ret[s, g, 0:rows, cols] = out[0:rows]
                inc[s, g, rows:, cols] = out[rows:]
            else:
                inc[s, g, 0:kept, cols] = out[0:kept]
                stag[s, :, cols] = out[kept:]
            return carry

        lax.fori_loop(0, half // tile, body, 0)
        if g == NEAR:
            for d in (2, 1, 3):
                yr_copy(s, h, g, d).start()
        else:
            for c in chunks(h):
                rs_copy(s, IN, 0, c).start()

    def join(s, h):
        for c in chunks(h):
            rs_copy(s, IN, 0, c).wait_recv()
            total = inc[s, FAR, 0:kept, chunk(c)].astype(jnp.float32) + jnp.dot(
                widen[...], swap[s, :, chunk(c)], preferred_element_type=jnp.float32
            )
            total = total.astype(jnp.bfloat16)
            ret[s, FAR, 0:pad, chunk(c)] = total[0:pad]
            inc[s, FAR, pad:kept, chunk(c)] = total[pad:]
        for d in (2, 1, 3):
            yr_copy(s, h, FAR, d).start()

    def rs_copy(s, way, step, c):
        if way == IN:
            src, dst = {
                0: (stag.at[s], swap.at[s]),
                2: (ag.at[s, 3], ag.at[s, 1]), 3: (tmp.at[s], ag.at[s, 0]),
            }[step]
        else:
            src, dst = {
                0: (pkd.at[s, 1], pkd.at[s, 2]), 1: (pkd.at[s, 0], pkd.at[s, 3]),
                2: (ag.at[s, 1], ag.at[s, 2]),
            }[step]
        return remote(
            src.at[:, chunk(c)], dst.at[:, chunk(c)],
            rs_send.at[s, way, step, c], rs_recv.at[s, way, step, c], zdev[way],
        )

    def near_rows(s, i, c):
        return jnp.dot(gmat[s, i], ret[s, NEAR, :, chunk(c)], preferred_element_type=jnp.float32)

    def far_rows(s, i, c):
        return jnp.dot(leaf[i], ret[s, FAR, 0:kept, chunk(c)], preferred_element_type=jnp.float32)

    def rs_begin(s, h):
        for step in (0, 1):
            for c in chunks(h):
                pkd[s, 1 - step, :, chunk(c)] = far_rows(s, 1 - step, c).astype(jnp.bfloat16)
                rs_copy(s, OUT, step, c).start()

    def spread_sum(s, step, c):
        own = near_rows(s, 3 - step, c)
        rs_copy(s, OUT, step, c).wait_recv()
        total = own + jnp.dot(
            spread[s, 1 - step], pkd[s, 2 + step, :, chunk(c)], preferred_element_type=jnp.float32
        )
        if step == 0:
            ag[s, 3, :, chunk(c)] = total.astype(jnp.bfloat16)
        else:
            tmp[s, :, chunk(c)] = total.astype(jnp.bfloat16)
        rs_copy(s, IN, 2 + step, c).start()

    def pass_sum(s, c):
        own = near_rows(s, 1, c)
        rs_copy(s, IN, 2, c).wait_recv()
        total = own + ag[s, 1, :, chunk(c)].astype(jnp.float32)
        ag[s, 1, :, chunk(c)] = total.astype(jnp.bfloat16)
        rs_copy(s, OUT, 2, c).start()

    def rs_two(s, h):
        for c in chunks(h):
            spread_sum(s, 0, c)

    def rs_one(s, h):
        for c in chunks(h):
            spread_sum(s, 1, c)

    def rs_pass(s, h):
        for c in chunks(h):
            pass_sum(s, c)

    def sh_copy(s, c):
        return remote(
            stage.at[s, :, chunk(c)], outs[s].at[:, chunk(c)], sh_send.at[s, c], sh_recv.at[s, c], pdev[s]
        )

    def rs_end(s, h):
        for c in chunks(h):
            own = near_rows(s, 0, c) + xs[s, :, chunk(c)].astype(jnp.float32)
            rs_copy(s, OUT, 2, c).wait_recv()
            rs_copy(s, IN, 3, c).wait_recv()
            total = own + (
                ag[s, 0, :, chunk(c)].astype(jnp.float32) + ag[s, 2, :, chunk(c)].astype(jnp.float32)
            )
            stage[s, :, chunk(c)] = total.astype(jnp.bfloat16)
            sh_copy(s, c).start()

    def finish(s):
        for h in (0, 1):
            for g in (0, 1):
                for d in (1, 2, 3):
                    yd_copy(s, h, g, d).wait_send()
                    yr_copy(s, h, g, d).wait_send()
        for c in range(4):
            for step in (0, 2, 3):
                rs_copy(s, IN, step, c).wait_send()
            for step in (0, 1, 2):
                rs_copy(s, OUT, step, c).wait_send()
            sh_copy(s, c).wait()

    def give_credit(s):
        gather_sent(s)
        for way in (IN, OUT):
            pl.semaphore_signal(credit.at[s], inc=1, device_id=zdev[way], device_id_type=MESH)

    f, r, near, far = 0, 1, NEAR, FAR
    both = (IN, OUT)

    load_xf.start()
    load_xr.start()
    own_info()
    load_xf.wait()
    normalise(f)
    pl.semaphore_wait(barrier, len(peers))

    inf_copy(0).start()
    inf_copy(1).start()
    own_send(f, 0, (IN,))
    own_send(f, 0, (OUT,))
    load_up.start()
    load_down.start()
    inf_copy(1).wait_recv()
    inf_copy(2).start()
    inf_copy(0).wait_recv()
    pack_matrices(0)
    second_hop(f, 0)
    own_send(f, 1, (OUT,))
    load_xr.wait()
    normalise(r)
    inf_copy(2).wait_recv()
    pack_matrices(1)
    third_hop(f, 0)
    select(f, 0, near)
    own_send(f, 1, (IN,))
    fourth_hop(f, 0)
    second_hop(f, 1)
    gather_end(f, 0)
    constants()
    select(f, 0, far)
    third_hop(f, 1)
    select(f, 1, near)
    own_send(r, 0, (OUT,))
    fourth_hop(f, 1)
    own_send(r, 0, (IN,))
    load_up.wait()
    load_down.wait()
    upper(f, 0, near)
    upper(f, 0, far)
    gather_end(f, 1)
    select(f, 1, far)
    own_send(r, 1, (IN,))
    upper(f, 1, near)
    give_credit(f)
    lower(f, 1, near)
    own_send(r, 1, (OUT,))
    second_hop(r, 0)
    second_hop(r, 1)
    upper(f, 1, far)
    lower(f, 0, far)
    lower(f, 1, far)
    lower(f, 0, near)
    third_hop(r, 1)
    third_hop(r, 0)
    select(r, 0, near)
    fourth_hop(r, 0)
    join(f, 0)
    back(f, 1, near)
    upper(r, 0, near)
    join(f, 1)
    back(f, 0, near)
    back(f, 0, far)
    select(r, 1, near)
    pl.semaphore_wait(credit.at[f], 2)
    rs_begin(f, 0)
    fourth_hop(r, 1)
    back(f, 1, far)
    rs_two(f, 0)
    rs_begin(f, 1)
    gather_end(r, 0)
    select(r, 0, far)
    gather_end(r, 1)
    select(r, 1, far)
    rs_two(f, 1)
    upper(r, 0, far)
    give_credit(r)
    rs_one(f, 1)
    upper(r, 1, near)
    upper(r, 1, far)
    lower(r, 0, far)
    lower(r, 0, near)
    lower(r, 1, far)
    rs_pass(f, 1)
    rs_one(f, 0)
    join(r, 0)
    rs_pass(f, 0)
    rs_end(f, 1)
    back(r, 0, far)
    pl.semaphore_wait(credit.at[r], 2)
    rs_begin(r, 0)
    join(r, 1)
    back(r, 0, near)
    rs_two(r, 0)
    lower(r, 1, near)
    rs_one(r, 0)
    back(r, 1, far)
    rs_begin(r, 1)
    rs_pass(r, 0)
    back(r, 1, near)
    rs_two(r, 1)
    rs_end(f, 0)
    rs_one(r, 1)
    rs_pass(r, 1)
    rs_end(r, 0)
    rs_end(r, 1)
    for i in range(len(INFO)):
        inf_copy(i).wait_send()
    finish(f)
    finish(r)


def settle(a_ref, b_ref, c_ref, d_ref, hold, into, out):
    rows = a_ref.shape[0] // 4
    steps = []
    for n, (source, target) in enumerate(((a_ref, c_ref), (b_ref, d_ref))):
        for i in range(4):
            at = pl.ds(i * rows, rows)
            first = pltpu.make_async_copy(source.at[at], hold.at[n, at], into.at[n, i])
            second = pltpu.make_async_copy(hold.at[n, at], target.at[at], out.at[n, i])
            first.start()
            steps.append((first, second))
    for first, second in steps:
        first.wait()
        second.start()
    for _, second in steps:
        second.wait()


def shards(stream_fwd, stream_rev, norm_gain, w_up, w_down, routes, gates):
    xf, xr = stream_fwd[0], stream_rev[0]
    upper, lower = w_up[0, 0], w_down[0, 0]
    tok, width = xf.shape
    hidden = upper.shape[1]
    experts = lax.axis_size("expert") // SPLIT
    cap = SPLIT * max(1, tok * TOPK * 5 // (4 * SPLIT * experts))
    info = jnp.concatenate([routes[0].astype(jnp.float32), gates[0].astype(jnp.float32)], axis=-1)
    info = info.transpose(0, 2, 1).reshape(8, tok)
    rows = GROUP * cap
    kept = NY * (-(-2 * cap // 16) * 16)
    bf16 = jnp.bfloat16
    dma = pltpu.SemaphoreType.DMA
    anywhere = pl.BlockSpec(memory_space=pl.ANY)
    in_vmem = pl.BlockSpec(memory_space=pltpu.VMEM)
    outf, outr = pl.pallas_call(
        functools.partial(kernel, cap),
        out_shape=(jax.ShapeDtypeStruct((tok, width), bf16),) * 2,
        in_specs=[anywhere, anywhere, in_vmem, anywhere, anywhere, in_vmem],
        out_specs=(anywhere, anywhere),
        scratch_shapes=[
            pltpu.VMEM((2, GROUP, tok, width), bf16),
            pltpu.VMEM((2, GROUP, NY * cap, width), bf16),
            pltpu.VMEM((2, 2 * NY * cap, width), bf16),
            pltpu.VMEM((2, 2 * NY * cap, width), bf16),
            pltpu.VMEM((2, tok, width), bf16),
            pltpu.VMEM((2, 2, NY * rows, width), bf16),
            pltpu.VMEM((2, 2, (NY - 1) * rows, width), bf16),
            pltpu.VMEM((2, 2, NY * rows, width), bf16),
            pltpu.VMEM((GROUP, 8, tok), jnp.float32),
            pltpu.VMEM((2, tok, width), bf16),
            pltpu.VMEM((2, tok, width), bf16),
            pltpu.VMEM((width, hidden), bf16),
            pltpu.VMEM((hidden, width), bf16),
            pltpu.VMEM((NY * rows, hidden), bf16),
            pltpu.VMEM((kept + 2 * NY * cap, hidden), bf16),
            pltpu.VMEM((2, NY * rows, hidden), jnp.float32),
            pltpu.VMEM((2, GROUP, tok, NY * rows), bf16),
            pltpu.VMEM((NY * rows, NY * rows), bf16),
            pltpu.VMEM((kept + 2 * NY * cap, NY * rows), bf16),
            pltpu.VMEM((kept, 2 * NY * cap), bf16),
            pltpu.VMEM((2, NY * cap, kept), bf16),
            pltpu.VMEM((2, 2, NY * cap, tok), bf16),
            pltpu.VMEM((2, 2, tok, NY * cap), bf16),
            dma((2, 2, 4, 4)), dma((2, 2, 4, 4)),
            dma((3,)), dma((3,)),
            dma((2, 2, 2, 3)), dma((2, 2, 2, 3)),
            dma((2, 2, 2, 3)), dma((2, 2, 2, 3)),
            dma((2, 2, 4, 4)), dma((2, 2, 4, 4)),
            dma((2, 4)), dma((2, 4)),
            dma((4,)),
            pltpu.SemaphoreType.REGULAR((2,)),
        ],
        compiler_params=pltpu.CompilerParams(
            collective_id=0, has_side_effects=True, vmem_limit_bytes=62 * 1024 * 1024
        ),
        cost_estimate=pl.CostEstimate(
            flops=2 * 2 * 2 * NZ * NY * cap * width * hidden,
            bytes_accessed=16 * 1024 * 1024,
            transcendentals=0,
        ),
    )(xf, xr, norm_gain, upper, lower, info)
    outf, outr = pl.pallas_call(
        settle,
        out_shape=(jax.ShapeDtypeStruct((tok, width), bf16),) * 2,
        in_specs=[anywhere, anywhere],
        out_specs=(anywhere, anywhere),
        scratch_shapes=[pltpu.VMEM((2, tok, width), bf16), dma((2, 4)), dma((2, 4))],
    )(outf, outr)
    return outf[None], outr[None]


def solution(mesh):
    return jax.shard_map(
        shards,
        mesh=mesh,
        in_specs=(
            P("pipe", "expert", None),
            P("pipe", "expert", None),
            P("pipe", None),
            P("pipe", "expert", None, None),
            P("pipe", "expert", None, None),
            P("pipe", None, "expert", None),
            P("pipe", None, "expert", None),
        ),
        out_specs=(P("pipe", "expert", None), P("pipe", "expert", None)),
        check_vma=False,
    )
```

```python
import functools

import jax
import jax.numpy as jnp
from jax import lax
from jax.experimental import pallas as pl
from jax.experimental.pallas import tpu as pltpu
from jax.sharding import PartitionSpec as P

SPLIT = 2
TOPK = 2
NY = 4
NZ = 8
GROUP = 4
MESH = pl.DeviceIdType.MESH

IN, OUT = 0, 1
NEAR, FAR = 0, 1
WIDE = ((0, 1), (1, 0))


def tile_of(width, most=512):
    tile = 128
    for t in range(128, most + 1, 128):
        if width % t == 0:
            tile = t
    return tile


def kernel(
    cap,
    xf_hbm, xr_hbm, gain_ref, up_hbm, down_hbm, picks_ref, gates_ref,
    outf_ref, outr_ref,
    ag, whole, pkd, stag, swap, tmp, inc, sel, ret, infos, xs, stage, up, down, act, parted, hid,
    gmat, order, order2, part, widen, leaf, pack, spread,
    ag_send, ag_recv, inf_send, inf_recv, yd_send, yd_recv, yr_send, yr_recv,
    rs_send, rs_recv, sh_send, sh_recv, load_sem, credit,
):
    tok, width = xs.shape[1], xs.shape[2]
    half = width // 2
    quarter = width // 4
    rows = GROUP * cap
    slots = NY * cap
    kept = parted.shape[0] - 2 * slots
    pad = kept // NY
    per_y = NZ // SPLIT
    experts = NY * per_y
    p = lax.axis_index("pipe")
    e = lax.axis_index("expert")
    n_pipe = lax.axis_size("pipe")
    y, z = e // NZ, e % NZ
    odd = z % 2
    z_in = z + 1 - 2 * odd
    z_out = (z + NZ - 1 + 2 * odd) % NZ
    zdev = {IN: (p, y * NZ + z_in), OUT: (p, y * NZ + z_out)}
    ydev = {d: (p, ((y + d) % NY) * NZ + z) for d in (1, 2, 3)}
    pdev = {0: ((p + 1) % n_pipe, e), 1: ((p + n_pipe - 1) % n_pipe, e)}
    outs = {0: outf_ref, 1: outr_ref}

    def remote(src, dst, send, recv, device):
        return pltpu.make_async_remote_copy(
            src_ref=src, dst_ref=dst, send_sem=send, recv_sem=recv,
            device_id=device, device_id_type=MESH,
        )

    def chunk(c):
        return pl.ds(c * quarter, quarter)

    barrier = pltpu.get_barrier_semaphore()
    peers = [zdev[0], zdev[1], ydev[1], ydev[2], ydev[3], pdev[0], pdev[1]]
    for device in peers:
        pl.semaphore_signal(barrier, inc=1, device_id=device, device_id_type=MESH)

    load_xf = pltpu.make_async_copy(xf_hbm, xs.at[0], load_sem.at[0])
    load_xr = pltpu.make_async_copy(xr_hbm, xs.at[1], load_sem.at[1])
    load_up = pltpu.make_async_copy(up_hbm, up, load_sem.at[2])
    load_down = pltpu.make_async_copy(down_hbm, down, load_sem.at[3])

    def normalise(s):
        gain = gain_ref[...].astype(jnp.float32)

        def body(i, carry):
            at = pl.ds(pl.multiple_of(i * 16, 16), 16)
            x = xs[s, at, :].astype(jnp.float32)
            scale = lax.rsqrt(jnp.mean(x * x, axis=-1, keepdims=True) + 1e-06)
            ag[s, 0, at, :] = (x * scale * gain).astype(jnp.bfloat16)
            return carry

        lax.fori_loop(0, tok // 16, body, 0)

    def own_info():
        here = lax.broadcasted_iota(jnp.int32, (experts, tok), 0).astype(jnp.float32)
        t0 = lax.broadcasted_iota(jnp.int32, (tok, tok), 0)
        t1 = lax.broadcasted_iota(jnp.int32, (tok, tok), 1)
        earlier = jnp.where(t0 < t1, 1.0, 0.0).astype(jnp.bfloat16)
        for s in (0, 1):
            picks = picks_ref[s].astype(jnp.float32)
            hits = [here == picks[k : k + 1, :] for k in range(TOPK)]
            named = jnp.where(hits[0] | hits[1], 1.0, 0.0).astype(jnp.bfloat16)
            before = jnp.dot(named, earlier, preferred_element_type=jnp.float32)
            for k in range(TOPK):
                code = jnp.where(hits[k], here * cap + before, 0.0)
                infos[0, 4 * s + k : 4 * s + k + 1, :] = jnp.sum(code, axis=0, keepdims=True)
            infos[0, 4 * s + 2 : 4 * s + 4, :] = gates_ref[s].astype(jnp.float32)

    def ag_copy(s, way, hop, c):
        packed = (stag.at[s, 0:slots], stag.at[s, slots : 2 * slots])
        if way == IN:
            plan = {
                1: (ag.at[s, 0], ag.at[s, 2]), 2: (ag.at[s, 1], ag.at[s, 3]),
                3: (pkd.at[s, 0], pkd.at[s, 2]), 4: (pkd.at[s, 1], pkd.at[s, 3]),
            }
            if (s, c // 2) in WIDE:
                plan[3] = (whole.at[s, 0], whole.at[s, 1])
        else:
            plan = {
                1: (ag.at[s, 0], ag.at[s, 1]), 2: (packed[0], pkd.at[s, 0]), 3: (packed[1], pkd.at[s, 1]),
            }
            if (s, c // 2) in WIDE:
                plan[2] = (ag.at[s, 2], whole.at[s, 0])
                plan[4] = (packed[0], pkd.at[s, 3])
        src, dst = plan[hop]
        return remote(
            src.at[:, chunk(c)], dst.at[:, chunk(c)],
            ag_send.at[s, way, hop - 1, c], ag_recv.at[s, way, hop - 1, c], zdev[way],
        )

    INFO = ((IN, 0, 2), (OUT, 0, 1), (IN, 1, 3), (OUT, 2, 4), (IN, 4, 5))

    def inf_copy(i):
        way, source, target = INFO[i]
        return remote(infos.at[source], infos.at[target], inf_send.at[i], inf_recv.at[i], zdev[way])

    def chunks(h):
        return (2 * h, 2 * h + 1)

    def own_send(s, h, ways):
        for c in chunks(h):
            for way in ways:
                ag_copy(s, way, 1, c).start()

    def pack_send(s, far, c):
        block = whole[s, 1, :, chunk(c)] if far == 2 else ag[s, 2 + far, :, chunk(c)]
        block = jnp.dot(pack[s, far], block, preferred_element_type=jnp.float32)
        at = far % 2 * slots
        stag[s, at : at + slots, chunk(c)] = block.astype(jnp.bfloat16)
        ag_copy(s, OUT, 2 + far, c).start()

    def second_hop(s, h):
        for c in chunks(h):
            ag_copy(s, OUT, 1, c).wait_recv()
            ag_copy(s, IN, 2, c).start()
            ag_copy(s, IN, 1, c).wait_recv()
            if (s, h) in WIDE:
                ag_copy(s, OUT, 2, c).start()
            else:
                pack_send(s, 0, c)

    def third_hop(s, h):
        for c in chunks(h):
            ag_copy(s, OUT, 2, c).wait_recv()
            ag_copy(s, IN, 3, c).start()
            ag_copy(s, IN, 2, c).wait_recv()
            pack_send(s, 1, c)

    def fourth_hop(s, h):
        for c in chunks(h):
            if (s, h) in WIDE:
                ag_copy(s, IN, 3, c).wait_recv()
                pack_send(s, 2, c)
            else:
                ag_copy(s, OUT, 3, c).wait_recv()
                ag_copy(s, IN, 4, c).start()

    def gather_end(s, h):
        for c in chunks(h):
            for hop in (3, 4):
                ag_copy(s, OUT if (s, h) in WIDE else IN, hop, c).wait_recv()

    def gather_sent(s):
        for c in range(4):
            last = OUT if (s, c // 2) in WIDE else IN
            for way in (IN, OUT):
                for hop in (1, 2, 3, 4) if way == last else (1, 2, 3):
                    ag_copy(s, way, hop, c).wait_send()

    def split_rows(shape):
        r = lax.broadcasted_iota(jnp.int32, shape, 0)
        one, zero = jnp.int32(1), jnp.int32(0)
        u = sum(jnp.where(r >= k * rows, one, zero) for k in (1, 2, 3))
        r = r - u * rows
        v = sum(jnp.where(r >= k * cap, one, zero) for k in (1, 2, 3))
        return u, v, r - v * cap

    def expert_at(d, pair):
        yd = y + d
        yd = yd - jnp.where(yd >= NY, jnp.int32(NY), jnp.int32(0))
        return yd * per_y + pair

    def constants():
        d, i, c = split_rows((NY * rows, NY * rows))
        column = lax.broadcasted_iota(jnp.int32, (NY * rows, NY * rows), 1)
        order[...] = jnp.where(column == i * slots + d * cap + c, 1.0, 0.0).astype(jnp.bfloat16)
        d, i, c = split_rows((NY * rows, 2 * slots))
        column = lax.broadcasted_iota(jnp.int32, (NY * rows, 2 * slots), 1)
        at = jnp.where(i == 1, 0, slots) + d * cap + c
        order2[...] = jnp.where((column == at) & ((i == 1) | (i == 3)), 1.0, 0.0).astype(jnp.bfloat16)
        r = lax.broadcasted_iota(jnp.int32, (kept, NY * rows), 0)
        column = lax.broadcasted_iota(jnp.int32, (kept, NY * rows), 1)
        d = sum(jnp.where(r >= k * pad, jnp.int32(1), jnp.int32(0)) for k in (1, 2, 3))
        q = r - d * pad
        part[0:kept] = jnp.where((column == d * rows + q) & (q < 2 * cap), 1.0, 0.0).astype(jnp.bfloat16)
        r = lax.broadcasted_iota(jnp.int32, (2 * slots, NY * rows), 0)
        column = lax.broadcasted_iota(jnp.int32, (2 * slots, NY * rows), 1)
        d = sum(jnp.where(r >= k * 2 * cap, jnp.int32(1), jnp.int32(0)) for k in (1, 2, 3))
        q = r - d * 2 * cap
        part[kept:] = jnp.where(column == d * rows + 2 * cap + q, 1.0, 0.0).astype(jnp.bfloat16)
        r = lax.broadcasted_iota(jnp.int32, (kept, 2 * slots), 0)
        column = lax.broadcasted_iota(jnp.int32, (kept, 2 * slots), 1)
        d = sum(jnp.where(r >= k * pad, jnp.int32(1), jnp.int32(0)) for k in (1, 2, 3))
        q = r - d * pad
        widen[...] = jnp.where((column == d * 2 * cap + q) & (q < 2 * cap), 1.0, 0.0).astype(jnp.bfloat16)
        _, d, c = split_rows((slots, kept))
        column = lax.broadcasted_iota(jnp.int32, (slots, kept), 1)
        for i in (0, 1):
            leaf[i] = jnp.where(column == d * pad + i * cap + c, 1.0, 0.0).astype(jnp.bfloat16)

    def hits_of(s, info, codes):
        hit0 = codes == info[4 * s : 4 * s + 1, :]
        hit1 = codes == info[4 * s + 1 : 4 * s + 2, :]
        weights = jnp.where(hit0, info[4 * s + 2 : 4 * s + 3, :], 0.0) + jnp.where(
            hit1, info[4 * s + 3 : 4 * s + 4, :], 0.0
        )
        return jnp.where(hit0 | hit1, 1.0, 0.0).astype(jnp.bfloat16), weights.T.astype(jnp.bfloat16)

    def pack_matrices(far):
        _, d, c = split_rows((slots, tok))
        codes = (expert_at(d, z_out // SPLIT) * cap + c).astype(jnp.float32)
        info = infos[2 + far if far < 2 else 5]
        for s in (0, 1):
            pack[s, far], weights = hits_of(s, info, codes)
            if far < 2:
                spread[s, far] = weights

    def select(s, h, g):
        if g == NEAR:
            d, at, c = split_rows((NY * rows, tok))
            codes = (expert_at(d, z // SPLIT) * cap + c).astype(jnp.float32)
            parts = []
            for i in range(GROUP):
                mine, weights = hits_of(s, infos[i], jnp.where(at == i, codes, -1.0))
                parts.append(mine)
                if h == 0:
                    gmat[s, i] = weights
            pick = jnp.concatenate(parts, axis=1)
        elif (s, h) in WIDE:
            d, at, c = split_rows((NY * rows, tok))
            codes = (expert_at(d, z // SPLIT) * cap + c).astype(jnp.float32)
            parts = [
                hits_of(s, infos[4 + n], jnp.where(at == 2 * n, codes, -1.0))[0] for n in (0, 1)
            ]
            pick = jnp.concatenate(parts, axis=1)
        tile = tile_of(half)

        def body(j, carry):
            cols = pl.ds(pl.multiple_of(h * half + j * tile, 128), tile)
            if g == NEAR:
                block = ag[s, :, :, cols].reshape(GROUP * tok, tile)
                out = jnp.dot(pick, block, preferred_element_type=jnp.float32)
            elif (s, h) in WIDE:
                block = whole[s, :, :, cols].reshape(2 * tok, tile)
                out = jnp.dot(pick, block, preferred_element_type=jnp.float32)
                block = jnp.concatenate([pkd[s, 1, :, cols], pkd[s, 3, :, cols]], axis=0)
                out = out + jnp.dot(order2[...], block, preferred_element_type=jnp.float32)
            else:
                block = pkd[s, :, :, cols].reshape(GROUP * slots, tile)
                out = jnp.dot(order[...], block, preferred_element_type=jnp.float32)
            out = out.astype(jnp.bfloat16)
            inc[s, g, 0:rows, cols] = out[0:rows]
            sel[s, g, :, cols] = out[rows:]
            return carry

        lax.fori_loop(0, half // tile, body, 0)
        for d in (1, 2, 3):
            yd_copy(s, h, g, d).start()

    def yd_copy(s, h, g, d):
        cols = pl.ds(h * half, half)
        return remote(
            sel.at[s, g, pl.ds((d - 1) * rows, rows), cols],
            inc.at[s, g, pl.ds(d * rows, rows), cols],
            yd_send.at[s, h, g, d - 1], yd_recv.at[s, h, g, d - 1], ydev[d],
        )

    def yr_copy(s, h, g, d):
        cols = pl.ds(h * half, half)
        many = rows if g == NEAR else pad
        block = pl.ds(d * many, many)
        return remote(
            inc.at[s, g, block, cols], ret.at[s, g, block, cols],
            yr_send.at[s, h, g, d - 1], yr_recv.at[s, h, g, d - 1], ydev[NY - d],
        )

    def back(s, h, g):
        for d in (1, 2, 3):
            yr_copy(s, h, g, d).wait_recv()

    def upper(s, h, g):
        for d in (1, 2, 3):
            yd_copy(s, h, g, d).wait_recv()
        tile = tile_of(half)
        if h == 0:
            hid[g] = jnp.zeros(hid.shape[1:], jnp.float32)

        def body(j, carry):
            cols = pl.ds(pl.multiple_of(h * half + j * tile, 128), tile)
            hid[g] += jnp.dot(inc[s, g, :, cols], up[cols, :], preferred_element_type=jnp.float32)
            return carry

        lax.fori_loop(0, half // tile, body, 0)
        if h == 1:
            value = jax.nn.silu(hid[g]).astype(jnp.bfloat16)
            if g == NEAR:
                act[...] = value
            else:
                parted[...] = jnp.dot(part[...], value, preferred_element_type=jnp.float32).astype(
                    jnp.bfloat16
                )

    def lower(s, h, g):
        tile = tile_of(half)

        def body(j, carry):
            cols = pl.ds(pl.multiple_of(h * half + j * tile, 128), tile)
            source = act if g == NEAR else parted
            out = jnp.dot(source[...], down[:, cols], preferred_element_type=jnp.float32)
            out = out.astype(jnp.bfloat16)
            if g == NEAR:
                ret[s, g, 0:rows, cols] = out[0:rows]
                inc[s, g, rows:, cols] = out[rows:]
            else:
                inc[s, g, 0:kept, cols] = out[0:kept]
                stag[s, :, cols] = out[kept:]
            return carry

        lax.fori_loop(0, half // tile, body, 0)
        if g == NEAR:
            for d in (2, 1, 3):
                yr_copy(s, h, g, d).start()
        else:
            for c in chunks(h):
                rs_copy(s, IN, 0, c).start()

    def join(s, h):
        for c in chunks(h):
            rs_copy(s, IN, 0, c).wait_recv()
            total = inc[s, FAR, 0:kept, chunk(c)].astype(jnp.float32) + jnp.dot(
                widen[...], swap[s, :, chunk(c)], preferred_element_type=jnp.float32
            )
            total = total.astype(jnp.bfloat16)
            ret[s, FAR, 0:pad, chunk(c)] = total[0:pad]
            inc[s, FAR, pad:kept, chunk(c)] = total[pad:]
        for d in (2, 1, 3):
            yr_copy(s, h, FAR, d).start()

    def rs_copy(s, way, step, c):
        if way == IN:
            src, dst = {
                0: (stag.at[s], swap.at[s]),
                2: (ag.at[s, 3], ag.at[s, 1]), 3: (tmp.at[s], ag.at[s, 0]),
            }[step]
        else:
            src, dst = {
                0: (pkd.at[s, 1], pkd.at[s, 2]), 1: (pkd.at[s, 0], pkd.at[s, 3]),
                2: (ag.at[s, 1], ag.at[s, 2]),
            }[step]
        return remote(
            src.at[:, chunk(c)], dst.at[:, chunk(c)],
            rs_send.at[s, way, step, c], rs_recv.at[s, way, step, c], zdev[way],
        )

    def near_rows(s, i, c):
        return jnp.dot(gmat[s, i], ret[s, NEAR, :, chunk(c)], preferred_element_type=jnp.float32)

    def far_rows(s, i, c):
        return jnp.dot(leaf[i], ret[s, FAR, 0:kept, chunk(c)], preferred_element_type=jnp.float32)

    def rs_begin(s, h):
        for step in (0, 1):
            for c in chunks(h):
                pkd[s, 1 - step, :, chunk(c)] = far_rows(s, 1 - step, c).astype(jnp.bfloat16)
                rs_copy(s, OUT, step, c).start()

    def spread_sum(s, step, c):
        own = near_rows(s, 3 - step, c)
        rs_copy(s, OUT, step, c).wait_recv()
        total = own + jnp.dot(
            spread[s, 1 - step], pkd[s, 2 + step, :, chunk(c)], preferred_element_type=jnp.float32
        )
        if step == 0:
            ag[s, 3, :, chunk(c)] = total.astype(jnp.bfloat16)
        else:
            tmp[s, :, chunk(c)] = total.astype(jnp.bfloat16)
        rs_copy(s, IN, 2 + step, c).start()

    def pass_sum(s, c):
        own = near_rows(s, 1, c)
        rs_copy(s, IN, 2, c).wait_recv()
        total = own + ag[s, 1, :, chunk(c)].astype(jnp.float32)
        ag[s, 1, :, chunk(c)] = total.astype(jnp.bfloat16)
        rs_copy(s, OUT, 2, c).start()

    def rs_two(s, h):
        for c in chunks(h):
            spread_sum(s, 0, c)

    def rs_one(s, h):
        for c in chunks(h):
            spread_sum(s, 1, c)

    def rs_pass(s, h):
        for c in chunks(h):
            pass_sum(s, c)

    def sh_copy(s, c):
        return remote(
            stage.at[s, :, chunk(c)], outs[s].at[:, chunk(c)], sh_send.at[s, c], sh_recv.at[s, c], pdev[s]
        )

    def rs_end(s, h):
        for c in chunks(h):
            own = near_rows(s, 0, c) + xs[s, :, chunk(c)].astype(jnp.float32)
            rs_copy(s, OUT, 2, c).wait_recv()
            rs_copy(s, IN, 3, c).wait_recv()
            total = own + (
                ag[s, 0, :, chunk(c)].astype(jnp.float32) + ag[s, 2, :, chunk(c)].astype(jnp.float32)
            )
            stage[s, :, chunk(c)] = total.astype(jnp.bfloat16)
            sh_copy(s, c).start()

    def finish(s):
        for h in (0, 1):
            for g in (0, 1):
                for d in (1, 2, 3):
                    yd_copy(s, h, g, d).wait_send()
                    yr_copy(s, h, g, d).wait_send()
        for c in range(4):
            for step in (0, 2, 3):
                rs_copy(s, IN, step, c).wait_send()
            for step in (0, 1, 2):
                rs_copy(s, OUT, step, c).wait_send()
            sh_copy(s, c).wait()

    def give_credit(s):
        gather_sent(s)
        for way in (IN, OUT):
            pl.semaphore_signal(credit.at[s], inc=1, device_id=zdev[way], device_id_type=MESH)

    f, r, near, far = 0, 1, NEAR, FAR
    both = (IN, OUT)

    load_xf.start()
    load_xr.start()
    own_info()
    load_xf.wait()
    normalise(f)
    pl.semaphore_wait(barrier, len(peers))

    inf_copy(0).start()
    inf_copy(1).start()
    own_send(f, 0, (IN,))
    own_send(f, 0, (OUT,))
    own_send(f, 1, (IN,))
    load_up.start()
    load_down.start()
    inf_copy(1).wait_recv()
    inf_copy(2).start()
    inf_copy(0).wait_recv()
    inf_copy(3).start()
    pack_matrices(0)
    constants()
    own_send(f, 1, (OUT,))
    second_hop(f, 0)
    second_hop(f, 1)
    inf_copy(2).wait_recv()
    inf_copy(3).wait_recv()
    inf_copy(4).start()
    pack_matrices(1)
    third_hop(f, 0)
    select(f, 0, near)
    fourth_hop(f, 0)
    inf_copy(4).wait_recv()
    pack_matrices(2)
    third_hop(f, 1)
    select(f, 1, near)
    load_xr.wait()
    normalise(r)
    own_send(r, 0, (OUT,))
    gather_end(f, 0)
    own_send(r, 1, (IN,))
    select(f, 0, far)
    fourth_hop(f, 1)
    load_up.wait()
    load_down.wait()
    upper(f, 0, near)
    gather_end(f, 1)
    upper(f, 1, near)
    own_send(r, 0, (IN,))
    select(f, 1, far)
    second_hop(r, 0)
    own_send(r, 1, (OUT,))
    lower(f, 0, near)
    give_credit(f)
    lower(f, 1, near)
    third_hop(r, 0)
    upper(f, 0, far)
    upper(f, 1, far)
    lower(f, 0, far)
    second_hop(r, 1)
    select(r, 0, near)
    fourth_hop(r, 0)
    join(f, 0)
    gather_end(r, 0)
    lower(f, 1, far)
    upper(r, 0, near)
    third_hop(r, 1)
    back(f, 0, near)
    select(r, 0, far)
    back(f, 0, far)
    fourth_hop(r, 1)
    join(f, 1)
    pl.semaphore_wait(credit.at[f], 2)
    rs_begin(f, 0)
    rs_two(f, 0)
    gather_end(r, 1)
    select(r, 1, far)
    upper(r, 0, far)
    back(f, 1, near)
    back(f, 1, far)
    rs_one(f, 0)
    rs_begin(f, 1)
    select(r, 1, near)
    rs_two(f, 1)
    give_credit(r)
    upper(r, 1, far)
    lower(r, 0, far)
    lower(r, 1, far)
    upper(r, 1, near)
    lower(r, 0, near)
    rs_pass(f, 0)
    rs_one(f, 1)
    join(r, 0)
    rs_pass(f, 1)
    rs_end(f, 0)
    join(r, 1)
    back(r, 0, far)
    back(r, 0, near)
    pl.semaphore_wait(credit.at[r], 2)
    rs_begin(r, 0)
    lower(r, 1, near)
    rs_two(r, 0)
    back(r, 1, far)
    rs_begin(r, 1)
    rs_one(r, 0)
    back(r, 1, near)
    rs_two(r, 1)
    rs_pass(r, 0)
    rs_one(r, 1)
    rs_pass(r, 1)
    rs_end(r, 0)
    rs_end(f, 1)
    rs_end(r, 1)
    for i in range(len(INFO)):
        inf_copy(i).wait_send()
    finish(f)
    finish(r)


def settle(a_ref, b_ref, c_ref, d_ref, hold, into, out):
    rows = a_ref.shape[0] // 4
    steps = []
    for n, (source, target) in enumerate(((a_ref, c_ref), (b_ref, d_ref))):
        for i in range(4):
            at = pl.ds(i * rows, rows)
            first = pltpu.make_async_copy(source.at[at], hold.at[n, at], into.at[n, i])
            second = pltpu.make_async_copy(hold.at[n, at], target.at[at], out.at[n, i])
            first.start()
            steps.append((first, second))
    for first, second in steps:
        first.wait()
        second.start()
    for _, second in steps:
        second.wait()


def shards(stream_fwd, stream_rev, norm_gain, w_up, w_down, routes, gates):
    xf, xr = stream_fwd[0], stream_rev[0]
    upper, lower = w_up[0, 0], w_down[0, 0]
    tok, width = xf.shape
    hidden = upper.shape[1]
    experts = lax.axis_size("expert") // SPLIT
    cap = SPLIT * max(1, tok * TOPK * 5 // (4 * SPLIT * experts))
    picks, weights = routes[0].transpose(0, 2, 1), gates[0].transpose(0, 2, 1)
    rows = GROUP * cap
    kept = NY * (-(-2 * cap // 16) * 16)
    bf16 = jnp.bfloat16
    dma = pltpu.SemaphoreType.DMA
    anywhere = pl.BlockSpec(memory_space=pl.ANY)
    in_vmem = pl.BlockSpec(memory_space=pltpu.VMEM)
    outf, outr = pl.pallas_call(
        functools.partial(kernel, cap),
        out_shape=(jax.ShapeDtypeStruct((tok, width), bf16),) * 2,
        in_specs=[anywhere, anywhere, in_vmem, anywhere, anywhere, in_vmem, in_vmem],
        out_specs=(anywhere, anywhere),
        scratch_shapes=[
            pltpu.VMEM((2, GROUP, tok, width), bf16),
            pltpu.VMEM((2, 2, tok, width), bf16),
            pltpu.VMEM((2, GROUP, NY * cap, width), bf16),
            pltpu.VMEM((2, 2 * NY * cap, width), bf16),
            pltpu.VMEM((2, 2 * NY * cap, width), bf16),
            pltpu.VMEM((2, tok, width), bf16),
            pltpu.VMEM((2, 2, NY * rows, width), bf16),
            pltpu.VMEM((2, 2, (NY - 1) * rows, width), bf16),
            pltpu.VMEM((2, 2, NY * rows, width), bf16),
            pltpu.VMEM((6, 8, tok), jnp.float32),
            pltpu.VMEM((2, tok, width), bf16),
            pltpu.VMEM((2, tok, width), bf16),
            pltpu.VMEM((width, hidden), bf16),
            pltpu.VMEM((hidden, width), bf16),
            pltpu.VMEM((NY * rows, hidden), bf16),
            pltpu.VMEM((kept + 2 * NY * cap, hidden), bf16),
            pltpu.VMEM((2, NY * rows, hidden), jnp.float32),
            pltpu.VMEM((2, GROUP, tok, NY * rows), bf16),
            pltpu.VMEM((NY * rows, NY * rows), bf16),
            pltpu.VMEM((NY * rows, 2 * NY * cap), bf16),
            pltpu.VMEM((kept + 2 * NY * cap, NY * rows), bf16),
            pltpu.VMEM((kept, 2 * NY * cap), bf16),
            pltpu.VMEM((2, NY * cap, kept), bf16),
            pltpu.VMEM((2, 3, NY * cap, tok), bf16),
            pltpu.VMEM((2, 2, tok, NY * cap), bf16),
            dma((2, 2, 4, 4)), dma((2, 2, 4, 4)),
            dma((5,)), dma((5,)),
            dma((2, 2, 2, 3)), dma((2, 2, 2, 3)),
            dma((2, 2, 2, 3)), dma((2, 2, 2, 3)),
            dma((2, 2, 4, 4)), dma((2, 2, 4, 4)),
            dma((2, 4)), dma((2, 4)),
            dma((4,)),
            pltpu.SemaphoreType.REGULAR((2,)),
        ],
        compiler_params=pltpu.CompilerParams(
            collective_id=0, has_side_effects=True, vmem_limit_bytes=62 * 1024 * 1024
        ),
        cost_estimate=pl.CostEstimate(
            flops=2 * 2 * 2 * NZ * NY * cap * width * hidden,
            bytes_accessed=16 * 1024 * 1024,
            transcendentals=0,
        ),
    )(xf, xr, norm_gain, upper, lower, picks, weights)
    outf, outr = pl.pallas_call(
        settle,
        out_shape=(jax.ShapeDtypeStruct((tok, width), bf16),) * 2,
        in_specs=[anywhere, anywhere],
        out_specs=(anywhere, anywhere),
        scratch_shapes=[pltpu.VMEM((2, tok, width), bf16), dma((2, 4)), dma((2, 4))],
    )(outf, outr)
    return outf[None], outr[None]


def solution(mesh):
    return jax.shard_map(
        shards,
        mesh=mesh,
        in_specs=(
            P("pipe", "expert", None),
            P("pipe", "expert", None),
            P("pipe", None),
            P("pipe", "expert", None, None),
            P("pipe", "expert", None, None),
            P("pipe", None, "expert", None),
            P("pipe", None, "expert", None),
        ),
        out_specs=(P("pipe", "expert", None), P("pipe", "expert", None)),
        check_vma=False,
    )
```

```python
import functools

import jax
import jax.numpy as jnp
from jax import lax
from jax.experimental import pallas as pl
from jax.experimental.pallas import tpu as pltpu
from jax.sharding import PartitionSpec as P

SPLIT = 2
TOPK = 2
NY = 4
NZ = 8
GROUP = 4
MESH = pl.DeviceIdType.MESH

IN, OUT = 0, 1
NEAR, FAR = 0, 1
WIDE = ((0, 1), (1, 0))


def tile_of(width, most=512):
    tile = 128
    for t in range(128, most + 1, 128):
        if width % t == 0:
            tile = t
    return tile


def kernel(
    cap,
    xf_hbm, xr_hbm, gain_ref, up_hbm, down_hbm, picks_ref, gates_ref,
    outf_ref, outr_ref,
    ag, whole, pkd, stag, swap, tmp, inc, sel, ret, infos, xs, stage, up, down, act, parted, hid,
    gmat, order, order2, part, widen, leaf, pack, spread,
    ag_send, ag_recv, inf_send, inf_recv, yd_send, yd_recv, yr_send, yr_recv,
    rs_send, rs_recv, sh_send, sh_recv, load_sem, credit,
):
    tok, width = xs.shape[1], xs.shape[2]
    half = width // 2
    quarter = width // 4
    rows = GROUP * cap
    slots = NY * cap
    kept = parted.shape[0] - 2 * slots
    pad = kept // NY
    per_y = NZ // SPLIT
    experts = NY * per_y
    p = lax.axis_index("pipe")
    e = lax.axis_index("expert")
    n_pipe = lax.axis_size("pipe")
    y, z = e // NZ, e % NZ
    odd = z % 2
    z_in = z + 1 - 2 * odd
    z_out = (z + NZ - 1 + 2 * odd) % NZ
    zdev = {IN: (p, y * NZ + z_in), OUT: (p, y * NZ + z_out)}
    ydev = {d: (p, ((y + d) % NY) * NZ + z) for d in (1, 2, 3)}
    pdev = {0: ((p + 1) % n_pipe, e), 1: ((p + n_pipe - 1) % n_pipe, e)}
    outs = {0: outf_ref, 1: outr_ref}

    def remote(src, dst, send, recv, device):
        return pltpu.make_async_remote_copy(
            src_ref=src, dst_ref=dst, send_sem=send, recv_sem=recv,
            device_id=device, device_id_type=MESH,
        )

    def chunk(c):
        return pl.ds(c * quarter, quarter)

    barrier = pltpu.get_barrier_semaphore()
    peers = [zdev[0], zdev[1], ydev[1], ydev[2], ydev[3], pdev[0], pdev[1]]
    for device in peers:
        pl.semaphore_signal(barrier, inc=1, device_id=device, device_id_type=MESH)

    load_xf = pltpu.make_async_copy(xf_hbm, xs.at[0], load_sem.at[0])
    load_xr = pltpu.make_async_copy(xr_hbm, xs.at[1], load_sem.at[1])
    load_up = pltpu.make_async_copy(up_hbm, up, load_sem.at[2])
    load_down = pltpu.make_async_copy(down_hbm, down, load_sem.at[3])

    def normalise(s):
        gain = gain_ref[...].astype(jnp.float32)

        def body(i, carry):
            at = pl.ds(pl.multiple_of(i * 16, 16), 16)
            x = xs[s, at, :].astype(jnp.float32)
            scale = lax.rsqrt(jnp.mean(x * x, axis=-1, keepdims=True) + 1e-06)
            ag[s, 0, at, :] = (x * scale * gain).astype(jnp.bfloat16)
            return carry

        lax.fori_loop(0, tok // 16, body, 0)

    def own_info():
        here = lax.broadcasted_iota(jnp.int32, (experts, tok), 0).astype(jnp.float32)
        t0 = lax.broadcasted_iota(jnp.int32, (tok, tok), 0)
        t1 = lax.broadcasted_iota(jnp.int32, (tok, tok), 1)
        earlier = jnp.where(t0 < t1, 1.0, 0.0).astype(jnp.bfloat16)
        for s in (0, 1):
            picks = picks_ref[s].astype(jnp.float32)
            hits = [here == picks[k : k + 1, :] for k in range(TOPK)]
            named = jnp.where(hits[0] | hits[1], 1.0, 0.0).astype(jnp.bfloat16)
            before = jnp.dot(named, earlier, preferred_element_type=jnp.float32)
            for k in range(TOPK):
                code = jnp.where(hits[k], here * cap + before, 0.0)
                infos[0, 4 * s + k : 4 * s + k + 1, :] = jnp.sum(code, axis=0, keepdims=True)
            infos[0, 4 * s + 2 : 4 * s + 4, :] = gates_ref[s].astype(jnp.float32)

    def ag_copy(s, way, hop, c):
        packed = (stag.at[s, 0:slots], stag.at[s, slots : 2 * slots])
        if way == IN:
            plan = {
                1: (ag.at[s, 0], ag.at[s, 2]), 2: (ag.at[s, 1], ag.at[s, 3]),
                3: (pkd.at[s, 0], pkd.at[s, 2]), 4: (pkd.at[s, 1], pkd.at[s, 3]),
            }
            if (s, c // 2) in WIDE:
                plan[3] = (whole.at[s, 0], whole.at[s, 1])
        else:
            plan = {
                1: (ag.at[s, 0], ag.at[s, 1]), 2: (packed[0], pkd.at[s, 0]), 3: (packed[1], pkd.at[s, 1]),
            }
            if (s, c // 2) in WIDE:
                plan[2] = (ag.at[s, 2], whole.at[s, 0])
                plan[4] = (packed[0], pkd.at[s, 3])
        src, dst = plan[hop]
        return remote(
            src.at[:, chunk(c)], dst.at[:, chunk(c)],
            ag_send.at[s, way, hop - 1, c], ag_recv.at[s, way, hop - 1, c], zdev[way],
        )

    INFO = ((IN, 0, 2), (OUT, 0, 1), (IN, 1, 3), (OUT, 2, 4), (IN, 4, 5))

    def inf_copy(i):
        way, source, target = INFO[i]
        return remote(infos.at[source], infos.at[target], inf_send.at[i], inf_recv.at[i], zdev[way])

    def chunks(h):
        return (2 * h, 2 * h + 1)

    cut = quarter // 256 * 128 + (quarter // 128) % 2 * 128

    def pieces(h):
        return (0, 1) if h == 0 else (2, 3, 4)

    def piece(c):
        if c < 3:
            return chunk(c)
        return pl.ds(3 * quarter, cut) if c == 3 else pl.ds(3 * quarter + cut, quarter - cut)

    def own_send(s, h, ways):
        for c in chunks(h):
            for way in ways:
                ag_copy(s, way, 1, c).start()

    def pack_send(s, far, c):
        block = whole[s, 1, :, chunk(c)] if far == 2 else ag[s, 2 + far, :, chunk(c)]
        block = jnp.dot(pack[s, far], block, preferred_element_type=jnp.float32)
        at = far % 2 * slots
        stag[s, at : at + slots, chunk(c)] = block.astype(jnp.bfloat16)
        ag_copy(s, OUT, 2 + far, c).start()

    def second_hop(s, h):
        for c in chunks(h):
            ag_copy(s, OUT, 1, c).wait_recv()
            ag_copy(s, IN, 2, c).start()
            ag_copy(s, IN, 1, c).wait_recv()
            if (s, h) in WIDE:
                ag_copy(s, OUT, 2, c).start()
            else:
                pack_send(s, 0, c)

    def third_hop(s, h):
        for c in chunks(h):
            ag_copy(s, OUT, 2, c).wait_recv()
            ag_copy(s, IN, 3, c).start()
            ag_copy(s, IN, 2, c).wait_recv()
            pack_send(s, 1, c)

    def fourth_hop(s, h):
        for c in chunks(h):
            if (s, h) in WIDE:
                ag_copy(s, IN, 3, c).wait_recv()
                pack_send(s, 2, c)
            else:
                ag_copy(s, OUT, 3, c).wait_recv()
                ag_copy(s, IN, 4, c).start()

    def gather_end(s, h):
        for c in chunks(h):
            for hop in (3, 4):
                ag_copy(s, OUT if (s, h) in WIDE else IN, hop, c).wait_recv()

    def gather_sent(s):
        for c in range(4):
            last = OUT if (s, c // 2) in WIDE else IN
            for way in (IN, OUT):
                for hop in (1, 2, 3, 4) if way == last else (1, 2, 3):
                    ag_copy(s, way, hop, c).wait_send()

    def split_rows(shape):
        r = lax.broadcasted_iota(jnp.int32, shape, 0)
        one, zero = jnp.int32(1), jnp.int32(0)
        u = sum(jnp.where(r >= k * rows, one, zero) for k in (1, 2, 3))
        r = r - u * rows
        v = sum(jnp.where(r >= k * cap, one, zero) for k in (1, 2, 3))
        return u, v, r - v * cap

    def expert_at(d, pair):
        yd = y + d
        yd = yd - jnp.where(yd >= NY, jnp.int32(NY), jnp.int32(0))
        return yd * per_y + pair

    def constants():
        d, i, c = split_rows((NY * rows, NY * rows))
        column = lax.broadcasted_iota(jnp.int32, (NY * rows, NY * rows), 1)
        order[...] = jnp.where(column == i * slots + d * cap + c, 1.0, 0.0).astype(jnp.bfloat16)
        d, i, c = split_rows((NY * rows, 2 * slots))
        column = lax.broadcasted_iota(jnp.int32, (NY * rows, 2 * slots), 1)
        at = jnp.where(i == 1, 0, slots) + d * cap + c
        order2[...] = jnp.where((column == at) & ((i == 1) | (i == 3)), 1.0, 0.0).astype(jnp.bfloat16)
        r = lax.broadcasted_iota(jnp.int32, (kept, NY * rows), 0)
        column = lax.broadcasted_iota(jnp.int32, (kept, NY * rows), 1)
        d = sum(jnp.where(r >= k * pad, jnp.int32(1), jnp.int32(0)) for k in (1, 2, 3))
        q = r - d * pad
        part[0:kept] = jnp.where((column == d * rows + q) & (q < 2 * cap), 1.0, 0.0).astype(jnp.bfloat16)
        r = lax.broadcasted_iota(jnp.int32, (2 * slots, NY * rows), 0)
        column = lax.broadcasted_iota(jnp.int32, (2 * slots, NY * rows), 1)
        d = sum(jnp.where(r >= k * 2 * cap, jnp.int32(1), jnp.int32(0)) for k in (1, 2, 3))
        q = r - d * 2 * cap
        part[kept:] = jnp.where(column == d * rows + 2 * cap + q, 1.0, 0.0).astype(jnp.bfloat16)
        r = lax.broadcasted_iota(jnp.int32, (kept, 2 * slots), 0)
        column = lax.broadcasted_iota(jnp.int32, (kept, 2 * slots), 1)
        d = sum(jnp.where(r >= k * pad, jnp.int32(1), jnp.int32(0)) for k in (1, 2, 3))
        q = r - d * pad
        widen[...] = jnp.where((column == d * 2 * cap + q) & (q < 2 * cap), 1.0, 0.0).astype(jnp.bfloat16)
        _, d, c = split_rows((slots, kept))
        column = lax.broadcasted_iota(jnp.int32, (slots, kept), 1)
        for i in (0, 1):
            leaf[i] = jnp.where(column == d * pad + i * cap + c, 1.0, 0.0).astype(jnp.bfloat16)

    def hits_of(s, info, codes):
        hit0 = codes == info[4 * s : 4 * s + 1, :]
        hit1 = codes == info[4 * s + 1 : 4 * s + 2, :]
        weights = jnp.where(hit0, info[4 * s + 2 : 4 * s + 3, :], 0.0) + jnp.where(
            hit1, info[4 * s + 3 : 4 * s + 4, :], 0.0
        )
        return jnp.where(hit0 | hit1, 1.0, 0.0).astype(jnp.bfloat16), weights.T.astype(jnp.bfloat16)

    def pack_matrices(far):
        _, d, c = split_rows((slots, tok))
        codes = (expert_at(d, z_out // SPLIT) * cap + c).astype(jnp.float32)
        info = infos[2 + far if far < 2 else 5]
        for s in (0, 1):
            pack[s, far], weights = hits_of(s, info, codes)
            if far < 2:
                spread[s, far] = weights

    def select(s, h, g):
        if g == NEAR:
            d, at, c = split_rows((NY * rows, tok))
            codes = (expert_at(d, z // SPLIT) * cap + c).astype(jnp.float32)
            parts = []
            for i in range(GROUP):
                mine, weights = hits_of(s, infos[i], jnp.where(at == i, codes, -1.0))
                parts.append(mine)
                if h == 0:
                    gmat[s, i] = weights
            pick = jnp.concatenate(parts, axis=1)
        elif (s, h) in WIDE:
            d, at, c = split_rows((NY * rows, tok))
            codes = (expert_at(d, z // SPLIT) * cap + c).astype(jnp.float32)
            parts = [
                hits_of(s, infos[4 + n], jnp.where(at == 2 * n, codes, -1.0))[0] for n in (0, 1)
            ]
            pick = jnp.concatenate(parts, axis=1)
        tile = tile_of(half)

        def body(j, carry):
            cols = pl.ds(pl.multiple_of(h * half + j * tile, 128), tile)
            if g == NEAR:
                block = ag[s, :, :, cols].reshape(GROUP * tok, tile)
                out = jnp.dot(pick, block, preferred_element_type=jnp.float32)
            elif (s, h) in WIDE:
                block = whole[s, :, :, cols].reshape(2 * tok, tile)
                out = jnp.dot(pick, block, preferred_element_type=jnp.float32)
                block = jnp.concatenate([pkd[s, 1, :, cols], pkd[s, 3, :, cols]], axis=0)
                out = out + jnp.dot(order2[...], block, preferred_element_type=jnp.float32)
            else:
                block = pkd[s, :, :, cols].reshape(GROUP * slots, tile)
                out = jnp.dot(order[...], block, preferred_element_type=jnp.float32)
            out = out.astype(jnp.bfloat16)
            inc[s, g, 0:rows, cols] = out[0:rows]
            sel[s, g, :, cols] = out[rows:]
            return carry

        lax.fori_loop(0, half // tile, body, 0)
        for d in (1, 2, 3):
            yd_copy(s, h, g, d).start()

    def yd_copy(s, h, g, d):
        cols = pl.ds(h * half, half)
        return remote(
            sel.at[s, g, pl.ds((d - 1) * rows, rows), cols],
            inc.at[s, g, pl.ds(d * rows, rows), cols],
            yd_send.at[s, h, g, d - 1], yd_recv.at[s, h, g, d - 1], ydev[d],
        )

    def yr_copy(s, h, g, d):
        cols = pl.ds(h * half, half)
        many = rows if g == NEAR else pad
        block = pl.ds(d * many, many)
        return remote(
            inc.at[s, g, block, cols], ret.at[s, g, block, cols],
            yr_send.at[s, h, g, d - 1], yr_recv.at[s, h, g, d - 1], ydev[NY - d],
        )

    def back(s, h, g):
        for d in (1, 2, 3):
            yr_copy(s, h, g, d).wait_recv()

    def upper(s, h, g):
        for d in (1, 2, 3):
            yd_copy(s, h, g, d).wait_recv()
        tile = tile_of(half)
        if h == 0:
            hid[g] = jnp.zeros(hid.shape[1:], jnp.float32)

        def body(j, carry):
            cols = pl.ds(pl.multiple_of(h * half + j * tile, 128), tile)
            hid[g] += jnp.dot(inc[s, g, :, cols], up[cols, :], preferred_element_type=jnp.float32)
            return carry

        lax.fori_loop(0, half // tile, body, 0)
        if h == 1:
            value = jax.nn.silu(hid[g]).astype(jnp.bfloat16)
            if g == NEAR:
                act[...] = value
            else:
                parted[...] = jnp.dot(part[...], value, preferred_element_type=jnp.float32).astype(
                    jnp.bfloat16
                )

    def lower(s, h, g):
        tile = tile_of(half)

        def body(j, carry):
            cols = pl.ds(pl.multiple_of(h * half + j * tile, 128), tile)
            source = act if g == NEAR else parted
            out = jnp.dot(source[...], down[:, cols], preferred_element_type=jnp.float32)
            out = out.astype(jnp.bfloat16)
            if g == NEAR:
                ret[s, g, 0:rows, cols] = out[0:rows]
                inc[s, g, rows:, cols] = out[rows:]
            else:
                inc[s, g, 0:kept, cols] = out[0:kept]
                stag[s, :, cols] = out[kept:]
            return carry

        lax.fori_loop(0, half // tile, body, 0)
        if g == NEAR:
            for d in (2, 1, 3):
                yr_copy(s, h, g, d).start()
        else:
            for c in pieces(h):
                rs_copy(s, IN, 0, c).start()

    def join(s, h):
        for c in pieces(h):
            rs_copy(s, IN, 0, c).wait_recv()
            total = inc[s, FAR, 0:kept, piece(c)].astype(jnp.float32) + jnp.dot(
                widen[...], swap[s, :, piece(c)], preferred_element_type=jnp.float32
            )
            total = total.astype(jnp.bfloat16)
            ret[s, FAR, 0:pad, piece(c)] = total[0:pad]
            inc[s, FAR, pad:kept, piece(c)] = total[pad:]
        for d in (2, 1, 3):
            yr_copy(s, h, FAR, d).start()

    def rs_copy(s, way, step, c):
        if way == IN:
            src, dst = {
                0: (stag.at[s], swap.at[s]),
                2: (ag.at[s, 3], ag.at[s, 1]), 3: (tmp.at[s], ag.at[s, 0]),
            }[step]
        else:
            src, dst = {
                0: (pkd.at[s, 1], pkd.at[s, 2]), 1: (pkd.at[s, 0], pkd.at[s, 3]),
                2: (ag.at[s, 1], ag.at[s, 2]),
            }[step]
        return remote(
            src.at[:, piece(c)], dst.at[:, piece(c)],
            rs_send.at[s, way, step, c], rs_recv.at[s, way, step, c], zdev[way],
        )

    def near_rows(s, i, c):
        return jnp.dot(gmat[s, i], ret[s, NEAR, :, piece(c)], preferred_element_type=jnp.float32)

    def far_rows(s, i, c):
        return jnp.dot(leaf[i], ret[s, FAR, 0:kept, piece(c)], preferred_element_type=jnp.float32)

    def rs_begin(s, h):
        for step in (0, 1):
            for c in pieces(h):
                pkd[s, 1 - step, :, piece(c)] = far_rows(s, 1 - step, c).astype(jnp.bfloat16)
                rs_copy(s, OUT, step, c).start()

    def spread_sum(s, step, c):
        own = near_rows(s, 3 - step, c)
        rs_copy(s, OUT, step, c).wait_recv()
        total = own + jnp.dot(
            spread[s, 1 - step], pkd[s, 2 + step, :, piece(c)], preferred_element_type=jnp.float32
        )
        if step == 0:
            ag[s, 3, :, piece(c)] = total.astype(jnp.bfloat16)
        else:
            tmp[s, :, piece(c)] = total.astype(jnp.bfloat16)
        rs_copy(s, IN, 2 + step, c).start()

    def pass_sum(s, c):
        own = near_rows(s, 1, c)
        rs_copy(s, IN, 2, c).wait_recv()
        total = own + ag[s, 1, :, piece(c)].astype(jnp.float32)
        ag[s, 1, :, piece(c)] = total.astype(jnp.bfloat16)
        rs_copy(s, OUT, 2, c).start()

    def rs_two(s, h):
        for c in pieces(h):
            spread_sum(s, 0, c)

    def rs_one(s, h):
        for c in pieces(h):
            spread_sum(s, 1, c)

    def rs_pass(s, h):
        for c in pieces(h):
            pass_sum(s, c)

    def sh_copy(s, c):
        return remote(
            stage.at[s, :, piece(c)], outs[s].at[:, piece(c)], sh_send.at[s, c], sh_recv.at[s, c], pdev[s]
        )

    def rs_end(s, h):
        for c in pieces(h):
            own = near_rows(s, 0, c) + xs[s, :, piece(c)].astype(jnp.float32)
            rs_copy(s, OUT, 2, c).wait_recv()
            rs_copy(s, IN, 3, c).wait_recv()
            total = own + (
                ag[s, 0, :, piece(c)].astype(jnp.float32) + ag[s, 2, :, piece(c)].astype(jnp.float32)
            )
            stage[s, :, piece(c)] = total.astype(jnp.bfloat16)
            sh_copy(s, c).start()

    def finish(s):
        for h in (0, 1):
            for g in (0, 1):
                for d in (1, 2, 3):
                    yd_copy(s, h, g, d).wait_send()
                    yr_copy(s, h, g, d).wait_send()
        for c in range(5):
            for step in (0, 2, 3):
                rs_copy(s, IN, step, c).wait_send()
            for step in (0, 1, 2):
                rs_copy(s, OUT, step, c).wait_send()
            sh_copy(s, c).wait()

    def give_credit(s):
        gather_sent(s)
        for way in (IN, OUT):
            pl.semaphore_signal(credit.at[s], inc=1, device_id=zdev[way], device_id_type=MESH)

    f, r, near, far = 0, 1, NEAR, FAR
    both = (IN, OUT)

    load_xf.start()
    load_xr.start()
    own_info()
    load_xf.wait()
    normalise(f)
    pl.semaphore_wait(barrier, len(peers))

    inf_copy(0).start()
    inf_copy(1).start()
    own_send(f, 0, (IN,))
    own_send(f, 0, (OUT,))
    own_send(f, 1, (OUT,))
    constants()
    load_up.start()
    load_down.start()
    inf_copy(1).wait_recv()
    inf_copy(2).start()
    inf_copy(0).wait_recv()
    inf_copy(3).start()
    pack_matrices(0)
    own_send(f, 1, (IN,))
    second_hop(f, 0)
    inf_copy(2).wait_recv()
    inf_copy(3).wait_recv()
    inf_copy(4).start()
    pack_matrices(1)
    second_hop(f, 1)
    third_hop(f, 0)
    select(f, 0, near)
    fourth_hop(f, 0)
    inf_copy(4).wait_recv()
    pack_matrices(2)
    third_hop(f, 1)
    load_xr.wait()
    normalise(r)
    own_send(r, 0, (IN,))
    select(f, 1, near)
    own_send(r, 0, (OUT,))
    gather_end(f, 0)
    own_send(r, 1, (IN,))
    select(f, 0, far)
    fourth_hop(f, 1)
    load_up.wait()
    load_down.wait()
    upper(f, 0, near)
    upper(f, 1, near)
    lower(f, 1, near)
    gather_end(f, 1)
    second_hop(r, 0)
    own_send(r, 1, (OUT,))
    select(f, 1, far)
    third_hop(r, 0)
    lower(f, 0, near)
    back(f, 1, near)
    second_hop(r, 1)
    give_credit(f)
    select(r, 0, near)
    upper(f, 0, far)
    fourth_hop(r, 0)
    upper(f, 1, far)
    lower(f, 0, far)
    third_hop(r, 1)
    gather_end(r, 0)
    fourth_hop(r, 1)
    lower(f, 1, far)
    join(f, 0)
    select(r, 0, far)
    back(f, 0, far)
    pl.semaphore_wait(credit.at[f], 2)
    rs_begin(f, 0)
    gather_end(r, 1)
    select(r, 1, far)
    back(f, 0, near)
    rs_two(f, 0)
    rs_one(f, 0)
    join(f, 1)
    select(r, 1, near)
    upper(r, 0, far)
    upper(r, 0, near)
    rs_pass(f, 0)
    give_credit(r)
    upper(r, 1, far)
    lower(r, 0, far)
    lower(r, 1, far)
    back(f, 1, far)
    rs_begin(f, 1)
    rs_end(f, 0)
    join(r, 0)
    upper(r, 1, near)
    lower(r, 0, near)
    rs_two(f, 1)
    back(r, 0, far)
    pl.semaphore_wait(credit.at[r], 2)
    rs_begin(r, 0)
    rs_one(f, 1)
    join(r, 1)
    rs_pass(f, 1)
    back(r, 0, near)
    lower(r, 1, near)
    rs_two(r, 0)
    rs_one(r, 0)
    back(r, 1, far)
    rs_begin(r, 1)
    rs_pass(r, 0)
    back(r, 1, near)
    rs_two(r, 1)
    rs_one(r, 1)
    rs_pass(r, 1)
    rs_end(r, 0)
    rs_end(f, 1)
    rs_end(r, 1)
    for i in range(len(INFO)):
        inf_copy(i).wait_send()
    finish(f)
    finish(r)


def shards(stream_fwd, stream_rev, norm_gain, w_up, w_down, routes, gates):
    xf, xr = stream_fwd[0], stream_rev[0]
    upper, lower = w_up[0, 0], w_down[0, 0]
    tok, width = xf.shape
    hidden = upper.shape[1]
    experts = lax.axis_size("expert") // SPLIT
    cap = SPLIT * max(1, tok * TOPK * 5 // (4 * SPLIT * experts))
    picks, weights = routes[0].transpose(0, 2, 1), gates[0].transpose(0, 2, 1)
    rows = GROUP * cap
    kept = NY * (-(-2 * cap // 16) * 16)
    bf16 = jnp.bfloat16
    dma = pltpu.SemaphoreType.DMA
    anywhere = pl.BlockSpec(memory_space=pl.ANY)
    in_vmem = pl.BlockSpec(memory_space=pltpu.VMEM)
    outf, outr = pl.pallas_call(
        functools.partial(kernel, cap),
        out_shape=(pltpu.VMEM((tok, width), bf16),) * 2,
        in_specs=[anywhere, anywhere, in_vmem, anywhere, anywhere, in_vmem, in_vmem],
        out_specs=(in_vmem, in_vmem),
        scratch_shapes=[
            pltpu.VMEM((2, GROUP, tok, width), bf16),
            pltpu.VMEM((2, 2, tok, width), bf16),
            pltpu.VMEM((2, GROUP, NY * cap, width), bf16),
            pltpu.VMEM((2, 2 * NY * cap, width), bf16),
            pltpu.VMEM((2, 2 * NY * cap, width), bf16),
            pltpu.VMEM((2, tok, width), bf16),
            pltpu.VMEM((2, 2, NY * rows, width), bf16),
            pltpu.VMEM((2, 2, (NY - 1) * rows, width), bf16),
            pltpu.VMEM((2, 2, NY * rows, width), bf16),
            pltpu.VMEM((6, 8, tok), jnp.float32),
            pltpu.VMEM((2, tok, width), bf16),
            pltpu.VMEM((2, tok, width), bf16),
            pltpu.VMEM((width, hidden), bf16),
            pltpu.VMEM((hidden, width), bf16),
            pltpu.VMEM((NY * rows, hidden), bf16),
            pltpu.VMEM((kept + 2 * NY * cap, hidden), bf16),
            pltpu.VMEM((2, NY * rows, hidden), jnp.float32),
            pltpu.VMEM((2, GROUP, tok, NY * rows), bf16),
            pltpu.VMEM((NY * rows, NY * rows), bf16),
            pltpu.VMEM((NY * rows, 2 * NY * cap), bf16),
            pltpu.VMEM((kept + 2 * NY * cap, NY * rows), bf16),
            pltpu.VMEM((kept, 2 * NY * cap), bf16),
            pltpu.VMEM((2, NY * cap, kept), bf16),
            pltpu.VMEM((2, 3, NY * cap, tok), bf16),
            pltpu.VMEM((2, 2, tok, NY * cap), bf16),
            dma((2, 2, 4, 4)), dma((2, 2, 4, 4)),
            dma((5,)), dma((5,)),
            dma((2, 2, 2, 3)), dma((2, 2, 2, 3)),
            dma((2, 2, 2, 3)), dma((2, 2, 2, 3)),
            dma((2, 2, 4, 5)), dma((2, 2, 4, 5)),
            dma((2, 5)), dma((2, 5)),
            dma((4,)),
            pltpu.SemaphoreType.REGULAR((2,)),
        ],
        compiler_params=pltpu.CompilerParams(
            collective_id=0, has_side_effects=True, vmem_limit_bytes=62 * 1024 * 1024
        ),
        cost_estimate=pl.CostEstimate(
            flops=2 * 2 * 2 * NZ * NY * cap * width * hidden,
            bytes_accessed=16 * 1024 * 1024,
            transcendentals=0,
        ),
    )(xf, xr, norm_gain, upper, lower, picks, weights)
    return outf[None], outr[None]


def solution(mesh):
    return jax.shard_map(
        shards,
        mesh=mesh,
        in_specs=(
            P("pipe", "expert", None),
            P("pipe", "expert", None),
            P("pipe", None),
            P("pipe", "expert", None, None),
            P("pipe", "expert", None, None),
            P("pipe", None, "expert", None),
            P("pipe", None, "expert", None),
        ),
        out_specs=(P("pipe", "expert", None), P("pipe", "expert", None)),
        check_vma=False,
    )
```

```python
import functools

import jax
import jax.numpy as jnp
from jax import lax
from jax.experimental import pallas as pl
from jax.experimental.pallas import tpu as pltpu
from jax.sharding import PartitionSpec as P

SPLIT = 2
TOPK = 2
NY = 4
NZ = 8
GROUP = 4
MESH = pl.DeviceIdType.MESH

IN, OUT = 0, 1
NEAR, FAR = 0, 1
WIDE = ((0, 1), (1, 0), (1, 1))


def tile_of(width, most=512):
    tile = 128
    for t in range(128, most + 1, 128):
        if width % t == 0:
            tile = t
    return tile


def kernel(
    cap,
    xf_hbm, xr_hbm, gain_ref, up_hbm, down_hbm, picks_ref, gates_ref,
    outf_ref, outr_ref,
    ag, whole, pkd, stag, swap, tmp, inc, sel, ret, infos, xs, stage, up, down, act, parted, hid,
    gmat, order, order2, part, widen, leaf, pack, spread,
    ag_send, ag_recv, inf_send, inf_recv, yd_send, yd_recv, yr_send, yr_recv,
    rs_send, rs_recv, sh_send, sh_recv, load_sem, credit,
):
    tok, width = xs.shape[1], xs.shape[2]
    half = width // 2
    quarter = width // 4
    rows = GROUP * cap
    slots = NY * cap
    kept = parted.shape[0] - 2 * slots
    pad = kept // NY
    per_y = NZ // SPLIT
    experts = NY * per_y
    p = lax.axis_index("pipe")
    e = lax.axis_index("expert")
    n_pipe = lax.axis_size("pipe")
    y, z = e // NZ, e % NZ
    odd = z % 2
    z_in = z + 1 - 2 * odd
    z_out = (z + NZ - 1 + 2 * odd) % NZ
    zdev = {IN: (p, y * NZ + z_in), OUT: (p, y * NZ + z_out)}
    ydev = {d: (p, ((y + d) % NY) * NZ + z) for d in (1, 2, 3)}
    pdev = {0: ((p + 1) % n_pipe, e), 1: ((p + n_pipe - 1) % n_pipe, e)}
    outs = {0: outf_ref, 1: outr_ref}

    def remote(src, dst, send, recv, device):
        return pltpu.make_async_remote_copy(
            src_ref=src, dst_ref=dst, send_sem=send, recv_sem=recv,
            device_id=device, device_id_type=MESH,
        )

    def chunk(c):
        return pl.ds(c * quarter, quarter)

    barrier = pltpu.get_barrier_semaphore()
    peers = [zdev[0], zdev[1], ydev[1], ydev[2], ydev[3], pdev[0], pdev[1]]
    for device in peers:
        pl.semaphore_signal(barrier, inc=1, device_id=device, device_id_type=MESH)

    load_xf = pltpu.make_async_copy(xf_hbm, xs.at[0], load_sem.at[0])
    load_xr = pltpu.make_async_copy(xr_hbm, xs.at[1], load_sem.at[1])
    load_up = pltpu.make_async_copy(up_hbm, up, load_sem.at[2])
    load_down = pltpu.make_async_copy(down_hbm, down, load_sem.at[3])

    def normalise(s):
        gain = gain_ref[...].astype(jnp.float32)

        def body(i, carry):
            at = pl.ds(pl.multiple_of(i * 16, 16), 16)
            x = xs[s, at, :].astype(jnp.float32)
            scale = lax.rsqrt(jnp.mean(x * x, axis=-1, keepdims=True) + 1e-06)
            ag[s, 0, at, :] = (x * scale * gain).astype(jnp.bfloat16)
            return carry

        lax.fori_loop(0, tok // 16, body, 0)

    def own_info():
        here = lax.broadcasted_iota(jnp.int32, (experts, tok), 0).astype(jnp.float32)
        t0 = lax.broadcasted_iota(jnp.int32, (tok, tok), 0)
        t1 = lax.broadcasted_iota(jnp.int32, (tok, tok), 1)
        earlier = jnp.where(t0 < t1, 1.0, 0.0).astype(jnp.bfloat16)
        for s in (0, 1):
            picks = picks_ref[s].astype(jnp.float32)
            hits = [here == picks[k : k + 1, :] for k in range(TOPK)]
            named = jnp.where(hits[0] | hits[1], 1.0, 0.0).astype(jnp.bfloat16)
            before = jnp.dot(named, earlier, preferred_element_type=jnp.float32)
            for k in range(TOPK):
                code = jnp.where(hits[k], here * cap + before, 0.0)
                infos[0, 4 * s + k : 4 * s + k + 1, :] = jnp.sum(code, axis=0, keepdims=True)
            infos[0, 4 * s + 2 : 4 * s + 4, :] = gates_ref[s].astype(jnp.float32)

    def ag_copy(s, way, hop, c):
        packed = (stag.at[s, 0:slots], stag.at[s, slots : 2 * slots])
        if way == IN:
            plan = {
                1: (ag.at[s, 0], ag.at[s, 2]), 2: (ag.at[s, 1], ag.at[s, 3]),
                3: (pkd.at[s, 0], pkd.at[s, 2]), 4: (pkd.at[s, 1], pkd.at[s, 3]),
            }
            if (s, c // 2) in WIDE:
                plan[3] = (whole.at[s, 0], whole.at[s, 1])
        else:
            plan = {
                1: (ag.at[s, 0], ag.at[s, 1]), 2: (packed[0], pkd.at[s, 0]), 3: (packed[1], pkd.at[s, 1]),
            }
            if (s, c // 2) in WIDE:
                plan[2] = (ag.at[s, 2], whole.at[s, 0])
                plan[4] = (packed[0], pkd.at[s, 3])
        src, dst = plan[hop]
        return remote(
            src.at[:, chunk(c)], dst.at[:, chunk(c)],
            ag_send.at[s, way, hop - 1, c], ag_recv.at[s, way, hop - 1, c], zdev[way],
        )

    INFO = ((IN, 0, 2), (OUT, 0, 1), (IN, 1, 3), (OUT, 2, 4), (IN, 4, 5))

    def inf_copy(i):
        way, source, target = INFO[i]
        return remote(infos.at[source], infos.at[target], inf_send.at[i], inf_recv.at[i], zdev[way])

    def chunks(h):
        return (2 * h, 2 * h + 1)

    cut = quarter // 256 * 128 + (quarter // 128) % 2 * 128

    def pieces(h):
        return (0, 1) if h == 0 else (2, 3, 4)

    def piece(c):
        if c < 3:
            return chunk(c)
        return pl.ds(3 * quarter, cut) if c == 3 else pl.ds(3 * quarter + cut, quarter - cut)

    def own_send(s, h, ways):
        for c in chunks(h):
            for way in ways:
                ag_copy(s, way, 1, c).start()

    def pack_send(s, far, c):
        block = whole[s, 1, :, chunk(c)] if far == 2 else ag[s, 2 + far, :, chunk(c)]
        block = jnp.dot(pack[s, far], block, preferred_element_type=jnp.float32)
        at = far % 2 * slots
        stag[s, at : at + slots, chunk(c)] = block.astype(jnp.bfloat16)
        ag_copy(s, OUT, 2 + far, c).start()

    def second_hop(s, h):
        for c in chunks(h):
            ag_copy(s, OUT, 1, c).wait_recv()
            ag_copy(s, IN, 2, c).start()
            ag_copy(s, IN, 1, c).wait_recv()
            if (s, h) in WIDE:
                ag_copy(s, OUT, 2, c).start()
            else:
                pack_send(s, 0, c)

    def third_hop(s, h):
        for c in chunks(h):
            ag_copy(s, OUT, 2, c).wait_recv()
            ag_copy(s, IN, 3, c).start()
            ag_copy(s, IN, 2, c).wait_recv()
            pack_send(s, 1, c)

    def fourth_hop(s, h):
        for c in chunks(h):
            if (s, h) in WIDE:
                ag_copy(s, IN, 3, c).wait_recv()
                pack_send(s, 2, c)
            else:
                ag_copy(s, OUT, 3, c).wait_recv()
                ag_copy(s, IN, 4, c).start()

    def gather_end(s, h):
        for c in chunks(h):
            for hop in (3, 4):
                ag_copy(s, OUT if (s, h) in WIDE else IN, hop, c).wait_recv()

    def gather_sent(s):
        for c in range(4):
            last = OUT if (s, c // 2) in WIDE else IN
            for way in (IN, OUT):
                for hop in (1, 2, 3, 4) if way == last else (1, 2, 3):
                    ag_copy(s, way, hop, c).wait_send()

    def split_rows(shape):
        r = lax.broadcasted_iota(jnp.int32, shape, 0)
        one, zero = jnp.int32(1), jnp.int32(0)
        u = sum(jnp.where(r >= k * rows, one, zero) for k in (1, 2, 3))
        r = r - u * rows
        v = sum(jnp.where(r >= k * cap, one, zero) for k in (1, 2, 3))
        return u, v, r - v * cap

    def expert_at(d, pair):
        yd = y + d
        yd = yd - jnp.where(yd >= NY, jnp.int32(NY), jnp.int32(0))
        return yd * per_y + pair

    def constants():
        d, i, c = split_rows((NY * rows, NY * rows))
        column = lax.broadcasted_iota(jnp.int32, (NY * rows, NY * rows), 1)
        order[...] = jnp.where(column == i * slots + d * cap + c, 1.0, 0.0).astype(jnp.bfloat16)
        d, i, c = split_rows((NY * rows, 2 * slots))
        column = lax.broadcasted_iota(jnp.int32, (NY * rows, 2 * slots), 1)
        at = jnp.where(i == 1, 0, slots) + d * cap + c
        order2[...] = jnp.where((column == at) & ((i == 1) | (i == 3)), 1.0, 0.0).astype(jnp.bfloat16)
        r = lax.broadcasted_iota(jnp.int32, (kept, NY * rows), 0)
        column = lax.broadcasted_iota(jnp.int32, (kept, NY * rows), 1)
        d = sum(jnp.where(r >= k * pad, jnp.int32(1), jnp.int32(0)) for k in (1, 2, 3))
        q = r - d * pad
        part[0:kept] = jnp.where((column == d * rows + q) & (q < 2 * cap), 1.0, 0.0).astype(jnp.bfloat16)
        r = lax.broadcasted_iota(jnp.int32, (2 * slots, NY * rows), 0)
        column = lax.broadcasted_iota(jnp.int32, (2 * slots, NY * rows), 1)
        d = sum(jnp.where(r >= k * 2 * cap, jnp.int32(1), jnp.int32(0)) for k in (1, 2, 3))
        q = r - d * 2 * cap
        part[kept:] = jnp.where(column == d * rows + 2 * cap + q, 1.0, 0.0).astype(jnp.bfloat16)
        r = lax.broadcasted_iota(jnp.int32, (kept, 2 * slots), 0)
        column = lax.broadcasted_iota(jnp.int32, (kept, 2 * slots), 1)
        d = sum(jnp.where(r >= k * pad, jnp.int32(1), jnp.int32(0)) for k in (1, 2, 3))
        q = r - d * pad
        widen[...] = jnp.where((column == d * 2 * cap + q) & (q < 2 * cap), 1.0, 0.0).astype(jnp.bfloat16)
        _, d, c = split_rows((slots, kept))
        column = lax.broadcasted_iota(jnp.int32, (slots, kept), 1)
        for i in (0, 1):
            leaf[i] = jnp.where(column == d * pad + i * cap + c, 1.0, 0.0).astype(jnp.bfloat16)

    def hits_of(s, info, codes):
        hit0 = codes == info[4 * s : 4 * s + 1, :]
        hit1 = codes == info[4 * s + 1 : 4 * s + 2, :]
        weights = jnp.where(hit0, info[4 * s + 2 : 4 * s + 3, :], 0.0) + jnp.where(
            hit1, info[4 * s + 3 : 4 * s + 4, :], 0.0
        )
        return jnp.where(hit0 | hit1, 1.0, 0.0).astype(jnp.bfloat16), weights.T.astype(jnp.bfloat16)

    def pack_matrices(far):
        _, d, c = split_rows((slots, tok))
        codes = (expert_at(d, z_out // SPLIT) * cap + c).astype(jnp.float32)
        info = infos[2 + far if far < 2 else 5]
        for s in (0, 1):
            pack[s, far], weights = hits_of(s, info, codes)
            if far < 2:
                spread[s, far] = weights

    def select(s, h, g):
        if g == NEAR:
            d, at, c = split_rows((NY * rows, tok))
            codes = (expert_at(d, z // SPLIT) * cap + c).astype(jnp.float32)
            parts = []
            for i in range(GROUP):
                mine, weights = hits_of(s, infos[i], jnp.where(at == i, codes, -1.0))
                parts.append(mine)
                if h == 0:
                    gmat[s, i] = weights
            pick = jnp.concatenate(parts, axis=1)
        elif (s, h) in WIDE:
            d, at, c = split_rows((NY * rows, tok))
            codes = (expert_at(d, z // SPLIT) * cap + c).astype(jnp.float32)
            parts = [
                hits_of(s, infos[4 + n], jnp.where(at == 2 * n, codes, -1.0))[0] for n in (0, 1)
            ]
            pick = jnp.concatenate(parts, axis=1)
        tile = tile_of(half)

        def body(j, carry):
            cols = pl.ds(pl.multiple_of(h * half + j * tile, 128), tile)
            if g == NEAR:
                block = ag[s, :, :, cols].reshape(GROUP * tok, tile)
                out = jnp.dot(pick, block, preferred_element_type=jnp.float32)
            elif (s, h) in WIDE:
                block = whole[s, :, :, cols].reshape(2 * tok, tile)
                out = jnp.dot(pick, block, preferred_element_type=jnp.float32)
                block = jnp.concatenate([pkd[s, 1, :, cols], pkd[s, 3, :, cols]], axis=0)
                out = out + jnp.dot(order2[...], block, preferred_element_type=jnp.float32)
            else:
                block = pkd[s, :, :, cols].reshape(GROUP * slots, tile)
                out = jnp.dot(order[...], block, preferred_element_type=jnp.float32)
            out = out.astype(jnp.bfloat16)
            inc[s, g, 0:rows, cols] = out[0:rows]
            sel[s, g, :, cols] = out[rows:]
            return carry

        lax.fori_loop(0, half // tile, body, 0)
        for d in (1, 2, 3):
            yd_copy(s, h, g, d).start()

    def yd_copy(s, h, g, d):
        cols = pl.ds(h * half, half)
        return remote(
            sel.at[s, g, pl.ds((d - 1) * rows, rows), cols],
            inc.at[s, g, pl.ds(d * rows, rows), cols],
            yd_send.at[s, h, g, d - 1], yd_recv.at[s, h, g, d - 1], ydev[d],
        )

    def yr_copy(s, h, g, d):
        cols = pl.ds(h * half, half)
        many = rows if g == NEAR else pad
        block = pl.ds(d * many, many)
        return remote(
            inc.at[s, g, block, cols], ret.at[s, g, block, cols],
            yr_send.at[s, h, g, d - 1], yr_recv.at[s, h, g, d - 1], ydev[NY - d],
        )

    def back(s, h, g):
        for d in (1, 2, 3):
            yr_copy(s, h, g, d).wait_recv()

    def upper(s, h, g):
        for d in (1, 2, 3):
            yd_copy(s, h, g, d).wait_recv()
        tile = tile_of(half)
        if h == 0:
            hid[g] = jnp.zeros(hid.shape[1:], jnp.float32)

        def body(j, carry):
            cols = pl.ds(pl.multiple_of(h * half + j * tile, 128), tile)
            hid[g] += jnp.dot(inc[s, g, :, cols], up[cols, :], preferred_element_type=jnp.float32)
            return carry

        lax.fori_loop(0, half // tile, body, 0)
        if h == 1:
            value = jax.nn.silu(hid[g]).astype(jnp.bfloat16)
            if g == NEAR:
                act[...] = value
            else:
                parted[...] = jnp.dot(part[...], value, preferred_element_type=jnp.float32).astype(
                    jnp.bfloat16
                )

    def lower(s, h, g):
        tile = tile_of(half)

        def body(j, carry):
            cols = pl.ds(pl.multiple_of(h * half + j * tile, 128), tile)
            source = act if g == NEAR else parted
            out = jnp.dot(source[...], down[:, cols], preferred_element_type=jnp.float32)
            out = out.astype(jnp.bfloat16)
            if g == NEAR:
                ret[s, g, 0:rows, cols] = out[0:rows]
                inc[s, g, rows:, cols] = out[rows:]
            else:
                inc[s, g, 0:kept, cols] = out[0:kept]
                stag[s, :, cols] = out[kept:]
            return carry

        lax.fori_loop(0, half // tile, body, 0)
        if g == NEAR:
            for d in (2, 1, 3):
                yr_copy(s, h, g, d).start()
        else:
            for c in pieces(h):
                rs_copy(s, IN, 0, c).start()

    def join(s, h):
        for c in pieces(h):
            rs_copy(s, IN, 0, c).wait_recv()
            total = inc[s, FAR, 0:kept, piece(c)].astype(jnp.float32) + jnp.dot(
                widen[...], swap[s, :, piece(c)], preferred_element_type=jnp.float32
            )
            total = total.astype(jnp.bfloat16)
            ret[s, FAR, 0:pad, piece(c)] = total[0:pad]
            inc[s, FAR, pad:kept, piece(c)] = total[pad:]
        for d in (2, 1, 3):
            yr_copy(s, h, FAR, d).start()

    def rs_copy(s, way, step, c):
        if way == IN:
            src, dst = {
                0: (stag.at[s], swap.at[s]),
                2: (ag.at[s, 3], ag.at[s, 1]), 3: (tmp.at[s], ag.at[s, 0]),
            }[step]
        else:
            src, dst = {
                0: (pkd.at[s, 1], pkd.at[s, 2]), 1: (pkd.at[s, 0], pkd.at[s, 3]),
                2: (ag.at[s, 1], ag.at[s, 2]),
            }[step]
        return remote(
            src.at[:, piece(c)], dst.at[:, piece(c)],
            rs_send.at[s, way, step, c], rs_recv.at[s, way, step, c], zdev[way],
        )

    def near_rows(s, i, c):
        return jnp.dot(gmat[s, i], ret[s, NEAR, :, piece(c)], preferred_element_type=jnp.float32)

    def far_rows(s, i, c):
        return jnp.dot(leaf[i], ret[s, FAR, 0:kept, piece(c)], preferred_element_type=jnp.float32)

    def rs_begin(s, h):
        for step in (0, 1):
            for c in pieces(h):
                pkd[s, 1 - step, :, piece(c)] = far_rows(s, 1 - step, c).astype(jnp.bfloat16)
                rs_copy(s, OUT, step, c).start()

    def spread_sum(s, step, c):
        own = near_rows(s, 3 - step, c)
        rs_copy(s, OUT, step, c).wait_recv()
        total = own + jnp.dot(
            spread[s, 1 - step], pkd[s, 2 + step, :, piece(c)], preferred_element_type=jnp.float32
        )
        if step == 0:
            ag[s, 3, :, piece(c)] = total.astype(jnp.bfloat16)
        else:
            tmp[s, :, piece(c)] = total.astype(jnp.bfloat16)
        rs_copy(s, IN, 2 + step, c).start()

    def pass_sum(s, c):
        own = near_rows(s, 1, c)
        rs_copy(s, IN, 2, c).wait_recv()
        total = own + ag[s, 1, :, piece(c)].astype(jnp.float32)
        ag[s, 1, :, piece(c)] = total.astype(jnp.bfloat16)
        rs_copy(s, OUT, 2, c).start()

    def rs_two(s, h):
        for c in pieces(h):
            spread_sum(s, 0, c)

    def rs_one(s, h):
        for c in pieces(h):
            spread_sum(s, 1, c)

    def rs_pass(s, h):
        for c in pieces(h):
            pass_sum(s, c)

    def sh_copy(s, c):
        return remote(
            stage.at[s, :, piece(c)], outs[s].at[:, piece(c)], sh_send.at[s, c], sh_recv.at[s, c], pdev[s]
        )

    def rs_end(s, h):
        for c in pieces(h):
            own = near_rows(s, 0, c) + xs[s, :, piece(c)].astype(jnp.float32)
            rs_copy(s, OUT, 2, c).wait_recv()
            rs_copy(s, IN, 3, c).wait_recv()
            total = own + (
                ag[s, 0, :, piece(c)].astype(jnp.float32) + ag[s, 2, :, piece(c)].astype(jnp.float32)
            )
            stage[s, :, piece(c)] = total.astype(jnp.bfloat16)
            sh_copy(s, c).start()

    def finish(s):
        for h in (0, 1):
            for g in (0, 1):
                for d in (1, 2, 3):
                    yd_copy(s, h, g, d).wait_send()
                    yr_copy(s, h, g, d).wait_send()
        for c in range(5):
            for step in (0, 2, 3):
                rs_copy(s, IN, step, c).wait_send()
            for step in (0, 1, 2):
                rs_copy(s, OUT, step, c).wait_send()
            sh_copy(s, c).wait()

    def give_credit(s):
        gather_sent(s)
        for way in (IN, OUT):
            pl.semaphore_signal(credit.at[s], inc=1, device_id=zdev[way], device_id_type=MESH)

    f, r, near, far = 0, 1, NEAR, FAR
    both = (IN, OUT)

    load_xf.start()
    load_xr.start()
    own_info()
    load_xf.wait()
    normalise(f)
    pl.semaphore_wait(barrier, len(peers))

    inf_copy(0).start()
    inf_copy(1).start()
    own_send(f, 0, (IN,))
    own_send(f, 0, (OUT,))
    load_up.start()
    load_down.start()
    inf_copy(1).wait_recv()
    inf_copy(2).start()
    inf_copy(0).wait_recv()
    inf_copy(3).start()
    pack_matrices(0)
    second_hop(f, 0)
    own_send(f, 1, (IN,))
    own_send(f, 1, (OUT,))
    constants()
    inf_copy(2).wait_recv()
    inf_copy(3).wait_recv()
    inf_copy(4).start()
    pack_matrices(1)
    third_hop(f, 0)
    load_xr.wait()
    normalise(r)
    second_hop(f, 1)
    fourth_hop(f, 0)
    select(f, 0, near)
    inf_copy(4).wait_recv()
    pack_matrices(2)
    third_hop(f, 1)
    own_send(r, 0, (OUT,))
    select(f, 1, near)
    own_send(r, 0, (IN,))
    load_up.wait()
    load_down.wait()
    upper(f, 0, near)
    gather_end(f, 0)
    select(f, 0, far)
    fourth_hop(f, 1)
    own_send(r, 1, (OUT,))
    upper(f, 1, near)
    second_hop(r, 0)
    gather_end(f, 1)
    lower(f, 0, near)
    select(f, 1, far)
    lower(f, 1, near)
    own_send(r, 1, (IN,))
    third_hop(r, 0)
    second_hop(r, 1)
    give_credit(f)
    fourth_hop(r, 0)
    upper(f, 0, far)
    upper(f, 1, far)
    select(r, 0, near)
    lower(f, 0, far)
    back(f, 1, near)
    third_hop(r, 1)
    lower(f, 1, far)
    gather_end(r, 0)
    join(f, 0)
    select(r, 0, far)
    back(f, 0, near)
    fourth_hop(r, 1)
    back(f, 0, far)
    pl.semaphore_wait(credit.at[f], 2)
    rs_begin(f, 0)
    gather_end(r, 1)
    select(r, 1, far)
    rs_two(f, 0)
    join(f, 1)
    upper(r, 0, far)
    select(r, 1, near)
    give_credit(r)
    rs_one(f, 0)
    upper(r, 1, far)
    lower(r, 0, far)
    upper(r, 0, near)
    back(f, 1, far)
    rs_begin(f, 1)
    rs_pass(f, 0)
    lower(r, 1, far)
    join(r, 0)
    upper(r, 1, near)
    lower(r, 0, near)
    rs_two(f, 1)
    join(r, 1)
    back(r, 0, far)
    pl.semaphore_wait(credit.at[r], 2)
    rs_begin(r, 0)
    rs_one(f, 1)
    rs_pass(f, 1)
    lower(r, 1, near)
    back(r, 0, near)
    rs_end(f, 0)
    rs_two(r, 0)
    rs_one(r, 0)
    back(r, 1, far)
    rs_begin(r, 1)
    back(r, 1, near)
    rs_pass(r, 0)
    rs_two(r, 1)
    rs_end(f, 1)
    rs_one(r, 1)
    rs_pass(r, 1)
    rs_end(r, 0)
    rs_end(r, 1)
    for i in range(len(INFO)):
        inf_copy(i).wait_send()
    finish(f)
    finish(r)


def shards(stream_fwd, stream_rev, norm_gain, w_up, w_down, routes, gates):
    xf, xr = stream_fwd[0], stream_rev[0]
    upper, lower = w_up[0, 0], w_down[0, 0]
    tok, width = xf.shape
    hidden = upper.shape[1]
    experts = lax.axis_size("expert") // SPLIT
    cap = SPLIT * max(1, tok * TOPK * 5 // (4 * SPLIT * experts))
    picks, weights = routes[0].transpose(0, 2, 1), gates[0].transpose(0, 2, 1)
    rows = GROUP * cap
    kept = NY * (-(-2 * cap // 16) * 16)
    bf16 = jnp.bfloat16
    dma = pltpu.SemaphoreType.DMA
    anywhere = pl.BlockSpec(memory_space=pl.ANY)
    in_vmem = pl.BlockSpec(memory_space=pltpu.VMEM)
    outf, outr = pl.pallas_call(
        functools.partial(kernel, cap),
        out_shape=(pltpu.VMEM((tok, width), bf16),) * 2,
        in_specs=[anywhere, anywhere, in_vmem, anywhere, anywhere, in_vmem, in_vmem],
        out_specs=(in_vmem, in_vmem),
        scratch_shapes=[
            pltpu.VMEM((2, GROUP, tok, width), bf16),
            pltpu.VMEM((2, 2, tok, width), bf16),
            pltpu.VMEM((2, GROUP, NY * cap, width), bf16),
            pltpu.VMEM((2, 2 * NY * cap, width), bf16),
            pltpu.VMEM((2, 2 * NY * cap, width), bf16),
            pltpu.VMEM((2, tok, width), bf16),
            pltpu.VMEM((2, 2, NY * rows, width), bf16),
            pltpu.VMEM((2, 2, (NY - 1) * rows, width), bf16),
            pltpu.VMEM((2, 2, NY * rows, width), bf16),
            pltpu.VMEM((6, 8, tok), jnp.float32),
            pltpu.VMEM((2, tok, width), bf16),
            pltpu.VMEM((2, tok, width), bf16),
            pltpu.VMEM((width, hidden), bf16),
            pltpu.VMEM((hidden, width), bf16),
            pltpu.VMEM((NY * rows, hidden), bf16),
            pltpu.VMEM((kept + 2 * NY * cap, hidden), bf16),
            pltpu.VMEM((2, NY * rows, hidden), jnp.float32),
            pltpu.VMEM((2, GROUP, tok, NY * rows), bf16),
            pltpu.VMEM((NY * rows, NY * rows), bf16),
            pltpu.VMEM((NY * rows, 2 * NY * cap), bf16),
            pltpu.VMEM((kept + 2 * NY * cap, NY * rows), bf16),
            pltpu.VMEM((kept, 2 * NY * cap), bf16),
            pltpu.VMEM((2, NY * cap, kept), bf16),
            pltpu.VMEM((2, 3, NY * cap, tok), bf16),
            pltpu.VMEM((2, 2, tok, NY * cap), bf16),
            dma((2, 2, 4, 4)), dma((2, 2, 4, 4)),
            dma((5,)), dma((5,)),
            dma((2, 2, 2, 3)), dma((2, 2, 2, 3)),
            dma((2, 2, 2, 3)), dma((2, 2, 2, 3)),
            dma((2, 2, 4, 5)), dma((2, 2, 4, 5)),
            dma((2, 5)), dma((2, 5)),
            dma((4,)),
            pltpu.SemaphoreType.REGULAR((2,)),
        ],
        compiler_params=pltpu.CompilerParams(
            collective_id=0, has_side_effects=True, vmem_limit_bytes=62 * 1024 * 1024
        ),
        cost_estimate=pl.CostEstimate(
            flops=2 * 2 * 2 * NZ * NY * cap * width * hidden,
            bytes_accessed=16 * 1024 * 1024,
            transcendentals=0,
        ),
    )(xf, xr, norm_gain, upper, lower, picks, weights)
    return outf[None], outr[None]


def solution(mesh):
    return jax.shard_map(
        shards,
        mesh=mesh,
        in_specs=(
            P("pipe", "expert", None),
            P("pipe", "expert", None),
            P("pipe", None),
            P("pipe", "expert", None, None),
            P("pipe", "expert", None, None),
            P("pipe", None, "expert", None),
            P("pipe", None, "expert", None),
        ),
        out_specs=(P("pipe", "expert", None), P("pipe", "expert", None)),
        check_vma=False,
    )
```
